512 devices in a mesh: dp: 8 (over z_lo, x), fsdp: 16 (over y, core), tensor: 4 (over z_hi).
Axes of the slice: x: 4, y: 8, z: 8 (z_hi: 4, z_lo: 2; z = z_hi * 2 + z_lo), core: 2. Of those that a mesh axis runs over, the one named last changes fastest.
Arguments:
- activations: bfloat16 [8192, 16384], P(('dp', 'fsdp', 'tensor')), may hold values from -6 to 6
- cotangent: bfloat16 [8192, 8192], P(('dp', 'fsdp'), 'tensor'), may hold values from -6 to 6
- left_root: bfloat16 [16, 8, 1024, 1024], P('fsdp', 'tensor', 'dp'), may hold values from -1 to 3
- right_root: bfloat16 [16, 8, 1024, 1024], P('fsdp', 'tensor', 'dp'), may hold values from -1 to 3
Outputs:
- left_stat: float32 [16, 8, 1024, 1024], P('fsdp', 'tensor', 'dp')
- right_stat: float32 [16, 8, 1024, 1024], P('fsdp', 'tensor', 'dp')
- update: bfloat16 [16, 8, 1024, 1024], P('fsdp', 'tensor', 'dp')
The draws below stay inside these ranges and needn't reach their ends.
All inputs are finite; a program needn't handle non-finite values.
Results may differ from the reference program's by a relative error of at most 0.02.
Values may be sent and summed in bfloat16 or wider, within the bound.
A program may use at most 64 MiB of HBM per device.

```python
import math
import jax
import jax.numpy as jnp
from jax import lax

D = 8192
FF = 16384
BLOCK = 1024
TOK_DEV = 64
TOKENS = 8192
N_DP = 8
N_FSDP = 16


def root_matrix(key, spread, low, high):
    row_blocks = FF // BLOCK
    col_blocks = D // BLOCK
    key_noise, key_diag = jax.random.split(key)
    normal_part = jax.random.normal(key_noise, (row_blocks, col_blocks, BLOCK, BLOCK), jnp.float32)
    symmetric = (normal_part + jnp.swapaxes(normal_part, 2, 3)) * (spread * BLOCK ** (-0.5))
    diagonal = jnp.exp(jax.random.uniform(key_diag, (row_blocks, col_blocks, BLOCK), jnp.float32, math.log(low), math.log(high)))
    rows_index = jnp.arange(BLOCK)[:, None]
    cols_index = jnp.arange(BLOCK)[None, :]
    identity = (rows_index == cols_index).astype(jnp.float32)
    return symmetric + identity * diagonal[..., :, None]


def draw_left_root(key, part):
    key = jax.random.fold_in(key, 11)
    return root_matrix(key, 0.25, 0.5, 2.0).astype(jnp.bfloat16)


def draw_right_root(key, part):
    key = jax.random.fold_in(key, 23)
    return root_matrix(key, 0.25, 0.5, 2.0).astype(jnp.bfloat16)


def shard_levels(rng, shape, pieces, least, largest):
    def one(axis_at, shards_of):
        steps = jax.random.uniform(jax.random.fold_in(jax.random.fold_in(rng, 6), axis_at), (shards_of,), jnp.float32, least / len(pieces), largest / len(pieces))
        return jnp.repeat(jnp.exp(steps), shape[axis_at] // shards_of).reshape((-1,) + (1,) * (len(shape) - axis_at - 1))

    loudness = one(*pieces[0])
    for cut in pieces[1:]:
        loudness = loudness * one(*cut)
    return loudness


def gaussian(stream_key, extent, scale, most, cuts=(), held_as=jnp.bfloat16):
    loudness = shard_levels(stream_key, extent, cuts, -0.22, 0.18) if cuts else 1.0
    values = jax.random.normal(stream_key, extent, jnp.float32) * scale * loudness
    return jnp.minimum(jnp.maximum(values, -most), most).astype(held_as)


def setup_inputs(seed: int = 0) -> dict:
    splits = jax.random.split(jax.random.key(seed), 5)
    activations = gaussian(splits[0], (TOKENS, FF), 1.0, 6.0, ((0, 512),))
    cotangent = gaussian(splits[1], (TOKENS, D), 1.0, 6.0, ((0, 128), (1, 4)))
    left_root = draw_left_root(jax.random.fold_in(splits[4], 71), 0)
    right_root = draw_right_root(jax.random.fold_in(splits[4], 71), 0)
    return dict(activations=activations, cotangent=cotangent, left_root=left_root, right_root=right_root)


def reference(activations, cotangent, left_root, right_root):
    factor = TOKENS ** -0.5
    group_rows = TOK_DEV * N_FSDP
    summed = jnp.zeros((FF, D), jnp.float32)
    for member in range(N_DP):
        hidden_part = activations[member * group_rows:(member + 1) * group_rows]
        cot_part = cotangent[member * group_rows:(member + 1) * group_rows]
        group_term = jnp.dot(hidden_part.T, cot_part, preferred_element_type=jnp.float32) * factor
        summed = summed + lax.optimization_barrier(group_term.astype(jnp.bfloat16)).astype(jnp.float32)
    gradient = summed.astype(jnp.bfloat16)
    row_blocks = FF // BLOCK
    col_blocks = D // BLOCK
    grad_blocks = gradient.reshape(row_blocks, BLOCK, col_blocks, BLOCK).transpose(0, 2, 1, 3).astype(jnp.float32)
    inverse_block = 1.0 / BLOCK
    left_stat = jnp.einsum('rcik,rcjk->rcij', grad_blocks, grad_blocks) * inverse_block
    right_stat = jnp.einsum('rcki,rckj->rcij', grad_blocks, grad_blocks) * inverse_block
    lifted = jnp.einsum('rcik,rckj->rcij', left_root.astype(jnp.float32), grad_blocks).astype(jnp.bfloat16)
    update = jnp.einsum('rcik,rckj->rcij', lifted.astype(jnp.float32), right_root.astype(jnp.float32)).astype(jnp.bfloat16)
    return (left_stat, right_stat, update)
```

```python
import functools

import jax
import jax.numpy as jnp
from jax import lax
from jax.experimental import pallas as pl
from jax.experimental.pallas import tpu as pltpu
from jax.sharding import PartitionSpec as P

MESH = pl.DeviceIdType.MESH
X, Y, Z, CORES = 4, 8, 8, 2
F = Y * CORES
T = Z // 2
PIECE = 128
BLOCK = 1024
ROWS = 16
SLOT = F * ROWS
TILE = 256


def mod(value, size):
    return lax.rem(value + 2 * size, size)


def scaled(index, size):
    return pl.multiple_of(index * size, size)


def kernel(
    factor,
    a_ref, c_ref, lr_ref, rr_ref,
    left_ref, right_ref, upd_ref,
    a_buf, c_buf, g_buf, r_buf, l_buf, at_buf, t_buf, relay, near, gt_buf, lift_buf, o_buf,
    local_sem, swap_send, swap_recv,
    a_send, a_recv, c_send, c_recv, sib_send, sib_recv,
    z_send, z_recv, t_send, t_recv, g_send, g_recv, r_send, r_recv, o_send, o_recv,
):
    m = lax.axis_index("dp")
    f = lax.axis_index("fsdp")
    t = lax.axis_index("tensor")
    zl, x = lax.div(m, X), lax.rem(m, X)
    y, core = lax.div(f, CORES), lax.rem(f, CORES)
    z = 2 * t + zl
    other = 1 - zl

    def on_x(step):
        return (zl * X + mod(x + step, X), f, t)

    def on_y(step):
        return (m, mod(y + step, Y) * CORES + core, t)

    def on_z(step):
        there = mod(z + step, Z)
        return (lax.rem(there, 2) * X + x, f, lax.div(there, 2))

    def slot_of(there):
        return lax.rem(there, 2) * T + lax.div(there, 2)

    sibling = (m, y * CORES + 1 - core, t)
    partner = (other * X + x, f, t)
    sign = (1, -1)

    started = []

    def put(src, dst, send, recv, device):
        copy = pltpu.make_async_remote_copy(
            src_ref=src, dst_ref=dst, send_sem=send, recv_sem=recv,
            device_id=device, device_id_type=MESH,
        )
        copy.start()
        started.append(copy)

    def arrived(dst, recv):
        pltpu.make_async_remote_copy(
            src_ref=dst, dst_ref=dst, send_sem=recv, recv_sem=recv,
            device_id=sibling, device_id_type=MESH,
        ).wait_recv()

    barrier = pltpu.get_barrier_semaphore()

    def greet(d, carry):
        pl.semaphore_signal(barrier, inc=1, device_id=(m, mod(f + d, F), t), device_id_type=MESH)
        return carry

    lax.fori_loop(1, F, greet, 0)
    for device in (on_x(1), on_x(-1), on_z(1), on_z(-1)):
        pl.semaphore_signal(barrier, inc=1, device_id=device, device_id_type=MESH)

    slot = slot_of(z)
    my_rows = scaled(f, ROWS)
    local = [
        pltpu.make_async_copy(
            a_ref.at[:, pl.ds(scaled(f, BLOCK), BLOCK)],
            a_buf.at[slot, pl.ds(my_rows, ROWS), :], local_sem.at[0]),
        pltpu.make_async_copy(
            c_ref.at[:, :, pl.ds(scaled(zl, BLOCK), BLOCK)],
            c_buf.at[pl.ds(zl * T, T), pl.ds(my_rows, ROWS), :], local_sem.at[1]),
        pltpu.make_async_copy(lr_ref.at[zl], l_buf.at[zl], local_sem.at[2]),
        pltpu.make_async_copy(rr_ref.at[zl], r_buf.at[zl, x], local_sem.at[3]),
    ]
    for copy in local:
        copy.start()
    pl.semaphore_wait(barrier, F - 1 + 4)

    def c_chunk(half, owner):
        return c_buf.at[pl.ds(half * T, T), pl.ds(scaled(owner, ROWS), ROWS), :]

    put(c_ref.at[:, :, pl.ds(scaled(other, BLOCK), BLOCK)], c_chunk(zl, f),
        swap_send.at[0], swap_recv.at[0], partner)

    def a_copy(d):
        to = mod(f + d, F)
        return pltpu.make_async_remote_copy(
            src_ref=a_ref.at[:, pl.ds(scaled(to, BLOCK), BLOCK)],
            dst_ref=a_buf.at[slot, pl.ds(my_rows, ROWS), :],
            send_sem=a_send.at[d], recv_sem=a_recv.at[d],
            device_id=(m, to, t), device_id_type=MESH)

    def a_start(d, carry):
        a_copy(d).start()
        return carry

    lax.fori_loop(1, F, a_start, 0)

    def c_share(src, half, owner, way, step):
        put(src, c_chunk(half, owner), sib_send.at[half, way, step], sib_recv.at[half, way, step], sibling)

    def c_first(src, half):
        for way in (0, 1):
            put(src, c_chunk(half, f), c_send.at[way, half, 0], c_recv.at[way, half, 1], on_y(sign[way]))
        c_share(src, half, f, 0, 0)

    def r_first(src, half):
        for way in (0, 1):
            put(src, r_buf.at[half, x], r_send.at[way, half, 0], r_recv.at[way, half, 1], on_x(sign[way]))

    c_first(c_ref.at[:, :, pl.ds(scaled(zl, BLOCK), BLOCK)], zl)
    r_first(rr_ref.at[zl], zl)
    put(rr_ref.at[other], r_buf.at[zl, x], swap_send.at[1], swap_recv.at[1], partner)
    put(lr_ref.at[other], l_buf.at[zl], swap_send.at[2], swap_recv.at[2], partner)
    arrived(c_chunk(other, f), swap_recv.at[0])
    c_first(c_chunk(other, f), other)

    def a_wait(d, carry):
        arrived(a_buf.at[slot, pl.ds(scaled(mod(f - d, F), ROWS), ROWS), :], a_recv.at[d])
        return carry

    local[0].wait()
    lax.fori_loop(1, F, a_wait, 0)

    target = (mod(x + 2, X), mod(x + 1, X), mod(x - 1, X), x)

    def lanes(part, half):
        return pl.ds(pl.multiple_of((half * X + target[part]) * PIECE, PIECE), PIECE)

    def z_put(part, half, way, step, owner):
        ref = a_buf.at[owner, :, lanes(part, half)]
        put(ref, ref, z_send.at[way, part, half, step], z_recv.at[way, part, half, step + 1], on_z(sign[way]))

    def z_first(part):
        for half in (0, 1):
            for way in (0, 1):
                z_put(part, half, way, 0, slot)

    def z_event(part, step):
        for half in (0, 1):
            for way in (0, 1):
                if step == Z // 2 and way != half:
                    continue
                owner = slot_of(mod(z - sign[way] * step, Z))
                arrived(a_buf.at[owner, :, lanes(part, half)], z_recv.at[way, part, half, step])
                if step < Z // 2 - 1 or (step == Z // 2 - 1 and way == half):
                    z_put(part, half, way, step, owner)

    def c_event(step):
        for half in (0, 1):
            for way in (0, 1):
                if step == Y // 2 and way != half:
                    continue
                owner = mod(y - sign[way] * step, Y) * CORES + core
                chunk = c_chunk(half, owner)
                arrived(chunk, c_recv.at[way, half, step])
                if step < Y // 2 - 1 or (step == Y // 2 - 1 and way == half):
                    put(chunk, chunk, c_send.at[way, half, step], c_recv.at[way, half, step + 1],
                        on_y(sign[way]))
                c_share(chunk, half, owner, way, step)

    def c_rest():
        for step in range(Y // 2 + 1):
            for half in (0, 1):
                for way in (0, 1):
                    if (step == Y // 2 and way != half) or (step == 0 and way == 1):
                        continue
                    owner = mod(y - sign[way] * step, Y) * CORES + 1 - core
                    arrived(c_chunk(half, owner), sib_recv.at[half, way, step])

    def x_ring(ref_of, send, recv, step):
        for half in (0, 1):
            for way in (0, 1):
                if step == X // 2 and way != half:
                    continue
                ref = ref_of(half, mod(x - sign[way] * step, X))
                arrived(ref, recv.at[way, half, step])
                if step < X // 2 - 1 or (step == X // 2 - 1 and way == half):
                    put(ref, ref, send.at[way, half, step], recv.at[way, half, step + 1], on_x(sign[way]))

    def r_chunk(half, owner):
        return r_buf.at[half, owner]

    def g_chunk(half, owner):
        return g_buf.at[pl.ds(pl.multiple_of((half * X + owner) * PIECE, PIECE), PIECE), :]

    def transpose(part):
        for half in (0, 1):
            for k in range(Z):
                at_buf[pl.ds(half * PIECE, PIECE), pl.ds(k * SLOT, SLOT)] = a_buf[k, :, lanes(part, half)].T

    def columns(n):
        return pl.ds(pl.multiple_of(n * TILE, TILE), TILE)

    def term_tile(part, n):
        cols = columns(n)
        value = jnp.dot(
            at_buf[...], c_buf[:, :, cols].reshape(Z * SLOT, TILE),
            preferred_element_type=jnp.float32,
        ) * factor
        upper, lower = value[:PIECE], value[PIECE:]
        if part == 1:
            upper = upper + relay[0, :, cols].astype(jnp.float32)
        if part == 2:
            lower = lower + relay[1, :, cols].astype(jnp.float32)
        if part == 3:
            upper = upper + near[0, 0, :, cols].astype(jnp.float32) + near[1, 0, :, cols].astype(jnp.float32)
            lower = lower + near[0, 1, :, cols].astype(jnp.float32) + near[1, 1, :, cols].astype(jnp.float32)
            g_chunk(0, x)[:, cols] = upper.astype(jnp.bfloat16)
            g_chunk(1, x)[:, cols] = lower.astype(jnp.bfloat16)
        else:
            t_buf[part, 0, :, cols] = upper.astype(jnp.bfloat16)
            t_buf[part, 1, :, cols] = lower.astype(jnp.bfloat16)

    def term_tiles(part, first, last):
        def body(n, carry):
            term_tile(part, n)
            return carry
        lax.fori_loop(first, last, body, 0)

    def x_before(part):
        if part == 1:
            arrived(relay.at[0], t_recv.at[0])
        if part == 2:
            arrived(relay.at[1], t_recv.at[1])
        if part == 3:
            arrived(near.at[0], t_recv.at[2])
            arrived(near.at[1], t_recv.at[3])

    def x_after(part):
        if part == 0:
            put(t_buf.at[0, 0], relay.at[0], t_send.at[0], t_recv.at[0], on_x(1))
            put(t_buf.at[0, 1], relay.at[1], t_send.at[1], t_recv.at[1], on_x(-1))
        if part == 1:
            put(t_buf.at[1], near.at[0], t_send.at[2], t_recv.at[2], on_x(1))
        if part == 2:
            put(t_buf.at[2], near.at[1], t_send.at[3], t_recv.at[3], on_x(-1))
        if part == 3:
            for half in (0, 1):
                for way in (0, 1):
                    put(g_chunk(half, x), g_chunk(half, x), g_send.at[way, half, 0],
                        g_recv.at[way, half, 1], on_x(sign[way]))

    z_first(0)
    z_first(1)
    arrived(r_chunk(other, x), swap_recv.at[1])
    r_first(r_chunk(other, x), other)
    z_event(0, 1)
    c_event(1)
    z_event(0, 2)
    c_event(2)
    z_event(0, 3)
    x_ring(r_chunk, r_send, r_recv, 1)
    c_event(3)
    z_event(0, 4)
    c_event(4)
    local[1].wait()
    c_rest()
    for part in range(4):
        if part < 2:
            z_first(part + 2)
        transpose(part)
        if part < 3:
            z_event(part + 1, 1)
        x_before(part)
        term_tiles(part, 0, 2)
        if part < 3:
            z_event(part + 1, 2)
        term_tiles(part, 2, 4)
        x_after(part)
        if part < 3:
            z_event(part + 1, 3)
            z_event(part + 1, 4)

    x_ring(g_chunk, g_send, g_recv, 1)
    local[2].wait()
    local[3].wait()
    arrived(l_buf.at[other], swap_recv.at[2])
    x_ring(r_chunk, r_send, r_recv, 2)
    x_ring(g_chunk, g_send, g_recv, 2)

    def own_rows(half):
        return g_chunk(half, x)[...]

    def own_lanes(half):
        return pl.ds(pl.multiple_of((half * X + x) * PIECE, PIECE), PIECE)

    for half in (0, 1):
        gt_buf[pl.ds(half * PIECE, PIECE), :] = g_buf[:, own_lanes(half)].T

    def keep(which, cols, value):
        value = value.astype(jnp.bfloat16)
        o_buf[which, 0, :, cols] = value[:PIECE]
        o_buf[which, 1, :, cols] = value[PIECE:]

    outs = (left_ref, right_ref, upd_ref)
    inverse = 1.0 / BLOCK

    def ship(which):
        put(o_buf.at[which, other], outs[which].at[zl], o_send.at[which], o_recv.at[which], partner)
        copy = pltpu.make_async_copy(o_buf.at[which, zl], outs[which].at[zl], local_sem.at[4 + which])
        copy.start()
        return copy

    def left_tile(n, carry):
        rows = jnp.concatenate([own_rows(0), own_rows(1)], axis=0)
        keep(0, columns(n), inverse * lax.dot_general(
            rows, g_buf[columns(n), :], (((1,), (1,)), ((), ())),
            preferred_element_type=jnp.float32))
        return carry

    def right_tile(n, carry):
        keep(1, columns(n), inverse * jnp.dot(
            gt_buf[...], g_buf[:, columns(n)], preferred_element_type=jnp.float32))
        return carry

    def lift_tile(n, carry):
        rows = l_buf[...].reshape(2 * PIECE, BLOCK)
        lift_buf[:, columns(n)] = jnp.dot(
            rows, g_buf[:, columns(n)], preferred_element_type=jnp.float32).astype(jnp.bfloat16)
        return carry

    def upd_tile(n, carry):
        keep(2, columns(n), jnp.dot(
            lift_buf[...], r_buf[:, :, :, columns(n)].reshape(BLOCK, TILE),
            preferred_element_type=jnp.float32))
        return carry

    tiles = BLOCK // TILE
    lax.fori_loop(0, tiles, left_tile, 0)
    kept = [ship(0)]
    lax.fori_loop(0, tiles, right_tile, 0)
    kept.append(ship(1))
    lax.fori_loop(0, tiles, lift_tile, 0)
    lax.fori_loop(0, tiles, upd_tile, 0)
    kept.append(ship(2))

    def a_drain(d, carry):
        a_copy(d).wait_send()
        return carry

    lax.fori_loop(1, F, a_drain, 0)
    for copy in started:
        copy.wait_send()
    for copy in kept:
        copy.wait()
    for which in range(3):
        arrived(outs[which].at[other], o_recv.at[which])


def on_device(activations, cotangent, left_root, right_root):
    tokens = cotangent.shape[0]
    factor = float(tokens * lax.axis_size("dp") * lax.axis_size("fsdp")) ** (-0.5)
    bf16 = jnp.bfloat16
    dma = pltpu.SemaphoreType.DMA
    anywhere = pl.BlockSpec(memory_space=pl.ANY)
    piece = jax.ShapeDtypeStruct((2, PIECE, BLOCK), bf16)
    left, right, update = pl.pallas_call(
        functools.partial(kernel, factor),
        out_shape=(piece, piece, piece),
        in_specs=[anywhere] * 4,
        out_specs=(anywhere,) * 3,
        scratch_shapes=[
            pltpu.VMEM((Z, SLOT, BLOCK), bf16),
            pltpu.VMEM((Z, SLOT, BLOCK), bf16),
            pltpu.VMEM((BLOCK, BLOCK), bf16),
            pltpu.VMEM((2, X, PIECE, BLOCK), bf16),
            pltpu.VMEM((2, PIECE, BLOCK), bf16),
            pltpu.VMEM((2 * PIECE, Z * SLOT), bf16),
            pltpu.VMEM((3, 2, PIECE, BLOCK), bf16),
            pltpu.VMEM((2, PIECE, BLOCK), bf16),
            pltpu.VMEM((2, 2, PIECE, BLOCK), bf16),
            pltpu.VMEM((2 * PIECE, BLOCK), bf16),
            pltpu.VMEM((2 * PIECE, BLOCK), bf16),
            pltpu.VMEM((3, 2, PIECE, BLOCK), bf16),
            dma((7,)), dma((3,)), dma((3,)),
            dma((F,)), dma((F,)),
            dma((2, 2, 5)), dma((2, 2, 5)), dma((2, 2, 5)), dma((2, 2, 5)),
            dma((2, 4, 2, 5)), dma((2, 4, 2, 5)),
            dma((4,)), dma((4,)),
            dma((2, 2, 3)), dma((2, 2, 3)),
            dma((2, 2, 3)), dma((2, 2, 3)),
            dma((3,)), dma((3,)),
        ],
        compiler_params=pltpu.CompilerParams(
            collective_id=0, has_side_effects=True, vmem_limit_bytes=48 * 1024 * 1024
        ),
        cost_estimate=pl.CostEstimate(
            flops=6 * 2**30, bytes_accessed=8 * 2**20, transcendentals=0),
    )(
        activations,
        cotangent.reshape(T, ROWS, 2 * BLOCK),
        left_root.reshape(2, PIECE, BLOCK),
        right_root.reshape(2, PIECE, BLOCK),
    )
    shape = left_root.shape
    return (
        left.reshape(shape).astype(jnp.float32),
        right.reshape(shape).astype(jnp.float32),
        update.reshape(shape),
    )


def solution(mesh):
    return jax.shard_map(
        on_device,
        mesh=mesh,
        in_specs=(
            P(("dp", "fsdp", "tensor"), None),
            P(("dp", "fsdp"), "tensor"),
            P("fsdp", "tensor", "dp", None),
            P("fsdp", "tensor", "dp", None),
        ),
        out_specs=(
            P("fsdp", "tensor", "dp", None),
            P("fsdp", "tensor", "dp", None),
            P("fsdp", "tensor", "dp", None),
        ),
        check_vma=False,
    )
```

```python
import functools

import jax
import jax.numpy as jnp
from jax import lax
from jax.experimental import pallas as pl
from jax.experimental.pallas import tpu as pltpu
from jax.sharding import PartitionSpec as P

MESH = pl.DeviceIdType.MESH
X, Y, Z, CORES = 4, 8, 8, 2
F = Y * CORES
T = Z // 2
PIECE = 128
BLOCK = 1024
HALF = BLOCK // 2
ROWS = 16
SLOT = F * ROWS
TILE = 256


def mod(value, size):
    return lax.rem(value + 2 * size, size)


def scaled(index, size):
    return pl.multiple_of(index * size, size)


def kernel(
    factor,
    a_ref, c_ref, lr_ref, rr_ref,
    left_ref, right_ref, upd_ref,
    stage, a_buf, c_buf, g_buf, r_buf, l_buf, at_buf, t_buf, relay, near, gt_buf, lift_buf,
    right_acc, lift_acc, o_buf,
    local_sem, swap_send, swap_recv,
    a_send, a_recv, c_send, c_recv, sib_send, sib_recv,
    z_send, z_recv, t_send, t_recv, g_send, g_recv, r_send, r_recv, o_send, o_recv,
):
    m = lax.axis_index("dp")
    f = lax.axis_index("fsdp")
    t = lax.axis_index("tensor")
    zl, x = lax.div(m, X), lax.rem(m, X)
    y, core = lax.div(f, CORES), lax.rem(f, CORES)
    z = 2 * t + zl
    other = 1 - zl

    def on_x(step):
        return (zl * X + mod(x + step, X), f, t)

    def on_y(step):
        return (m, mod(y + step, Y) * CORES + core, t)

    def on_z(step):
        there = mod(z + step, Z)
        return (lax.rem(there, 2) * X + x, f, lax.div(there, 2))

    def slot_of(there):
        return lax.rem(there, 2) * T + lax.div(there, 2)

    sibling = (m, y * CORES + 1 - core, t)
    partner = (other * X + x, f, t)
    sign = (1, -1)
    slot = slot_of(z)
    my_rows = scaled(f, ROWS)

    started = []

    def put(src, dst, send, recv, device):
        copy = pltpu.make_async_remote_copy(
            src_ref=src, dst_ref=dst, send_sem=send, recv_sem=recv,
            device_id=device, device_id_type=MESH,
        )
        copy.start()
        started.append(copy)

    def arrived(dst, recv):
        pltpu.make_async_remote_copy(
            src_ref=dst, dst_ref=dst, send_sem=recv, recv_sem=recv,
            device_id=sibling, device_id_type=MESH,
        ).wait_recv()

    barrier = pltpu.get_barrier_semaphore()

    def greet(d, carry):
        pl.semaphore_signal(barrier, inc=1, device_id=(m, mod(f + d, F), t), device_id_type=MESH)
        return carry

    for device in (on_z(1), on_z(-1), on_x(1), on_x(-1)):
        pl.semaphore_signal(barrier, inc=1, device_id=device, device_id_type=MESH)
    lax.fori_loop(1, F, greet, 0)

    local = [
        pltpu.make_async_copy(
            a_ref.at[:, pl.ds(scaled(f, BLOCK), BLOCK)],
            stage.at[pl.ds(my_rows, ROWS), :], local_sem.at[0]),
        pltpu.make_async_copy(
            c_ref.at[:, :, pl.ds(scaled(zl, BLOCK), BLOCK)],
            c_buf.at[pl.ds(zl * T, T), pl.ds(my_rows, ROWS), :], local_sem.at[1]),
        pltpu.make_async_copy(lr_ref.at[zl], l_buf.at[zl], local_sem.at[2]),
        pltpu.make_async_copy(rr_ref.at[zl], r_buf.at[zl, x], local_sem.at[3]),
    ]
    for copy in local:
        copy.start()
    pl.semaphore_wait(barrier, F - 1 + 4)

    def a_copy(part, d):
        to = mod(f + d, F)
        start = pl.multiple_of(to * BLOCK + part * HALF, HALF)
        return pltpu.make_async_remote_copy(
            src_ref=a_ref.at[:, pl.ds(start, HALF)],
            dst_ref=stage.at[pl.ds(my_rows, ROWS), pl.ds(part * HALF, HALF)],
            send_sem=a_send.at[part, d], recv_sem=a_recv.at[part, d],
            device_id=(m, to, t), device_id_type=MESH)

    def a_first(part):
        def body(d, carry):
            a_copy(part, d).start()
            return carry
        lax.fori_loop(1, F, body, 0)

    def a_event(part):
        def body(d, carry):
            rows = pl.ds(scaled(mod(f - d, F), ROWS), ROWS)
            arrived(stage.at[rows, pl.ds(part * HALF, HALF)], a_recv.at[part, d])
            return carry
        lax.fori_loop(1, F, body, 0)

    def a_drain(part):
        def body(d, carry):
            a_copy(part, d).wait_send()
            return carry
        lax.fori_loop(1, F, body, 0)

    def a_strips(part):
        for i in range(part * X, part * X + X):
            a_buf[i, slot] = stage[:, i * PIECE:(i + 1) * PIECE]

    def c_chunk(half, owner):
        return c_buf.at[pl.ds(half * T, T), pl.ds(scaled(owner, ROWS), ROWS), :]

    def c_share(src, half, owner, way, step):
        put(src, c_chunk(half, owner), sib_send.at[half, way, step], sib_recv.at[half, way, step], sibling)

    def c_first(src, half):
        for way in (0, 1):
            put(src, c_chunk(half, f), c_send.at[way, half, 0], c_recv.at[way, half, 1], on_y(sign[way]))
        c_share(src, half, f, 0, 0)

    def c_event(step):
        for half in (0, 1):
            for way in (0, 1):
                if step == Y // 2 and way != half:
                    continue
                owner = mod(y - sign[way] * step, Y) * CORES + core
                chunk = c_chunk(half, owner)
                arrived(chunk, c_recv.at[way, half, step])
                if step < Y // 2 - 1 or (step == Y // 2 - 1 and way == half):
                    put(chunk, chunk, c_send.at[way, half, step], c_recv.at[way, half, step + 1],
                        on_y(sign[way]))
                c_share(chunk, half, owner, way, step)

    def c_rest():
        for step in range(Y // 2 + 1):
            for half in (0, 1):
                for way in (0, 1):
                    if (step == Y // 2 and way != half) or (step == 0 and way == 1):
                        continue
                    owner = mod(y - sign[way] * step, Y) * CORES + 1 - core
                    arrived(c_chunk(half, owner), sib_recv.at[half, way, step])

    target = (mod(x + 2, X), mod(x + 1, X), mod(x - 1, X), x)

    def strip(j):
        return (j // X) * X + target[j % X]

    def z_put(j, way, step, owner):
        ref = a_buf.at[strip(j), owner]
        put(ref, ref, z_send.at[way, j, step], z_recv.at[way, j, step + 1], on_z(sign[way]))

    def z_first(j):
        for way in (0, 1):
            z_put(j, way, 0, slot)

    def z_event(j, step):
        for way in (0, 1):
            if step == Z // 2 and way != j % 2:
                continue
            owner = slot_of(mod(z - sign[way] * step, Z))
            arrived(a_buf.at[strip(j), owner], z_recv.at[way, j, step])
            if step < Z // 2 - 1 or (step == Z // 2 - 1 and way == j % 2):
                z_put(j, way, step, owner)

    def x_first(src_of, dst_of, send, recv, half):
        for way in (0, 1):
            put(src_of, dst_of, send.at[way, half, 0], recv.at[way, half, 1], on_x(sign[way]))

    def x_ring(ref_of, send, recv, step):
        for half in (0, 1):
            for way in (0, 1):
                if step == X // 2 and way != half:
                    continue
                ref = ref_of(half, mod(x - sign[way] * step, X))
                arrived(ref, recv.at[way, half, step])
                if step < X // 2 - 1 or (step == X // 2 - 1 and way == half):
                    put(ref, ref, send.at[way, half, step], recv.at[way, half, step + 1], on_x(sign[way]))

    def r_chunk(half, owner):
        return r_buf.at[half, owner]

    def r_first(src, half):
        x_first(src, r_chunk(half, x), r_send, r_recv, half)

    def r_event(step):
        x_ring(r_chunk, r_send, r_recv, step)

    def g_rows(h, owner):
        return pl.ds(pl.multiple_of((h * X + owner) * PIECE, PIECE), PIECE)

    def side(q):
        return pl.ds(q * HALF, HALF)

    def g_chunk(h):
        return lambda q, owner: g_buf.at[g_rows(h, owner), side(q)]

    def g_first(h, q):
        ref = g_chunk(h)(q, x)
        x_first(ref, ref, g_send.at[h], g_recv.at[h], q)

    def g_event(h, step):
        x_ring(g_chunk(h), g_send.at[h], g_recv.at[h], step)

    def columns(n):
        return pl.ds(pl.multiple_of(n * TILE, TILE), TILE)

    def turn(j):
        for k in range(Z):
            at_buf[j % X, :, pl.ds(k * SLOT, SLOT)] = a_buf[strip(j), k].T

    def multiply(j, q):
        h, part = j // X, j % X

        def body(n, carry):
            cols = columns(n)
            value = jnp.dot(
                at_buf[part], c_buf[:, :, cols].reshape(Z * SLOT, TILE),
                preferred_element_type=jnp.float32,
            ) * factor
            if (part, q) in ((1, 0), (2, 1)):
                value = value + relay[h, :, cols].astype(jnp.float32)
            if part == 3:
                value = value + near[h, 0, :, cols].astype(jnp.float32) + near[h, 1, :, cols].astype(jnp.float32)
                g_buf[g_rows(h, x), cols] = value.astype(jnp.bfloat16)
            else:
                t_buf[h, part, :, cols] = value.astype(jnp.bfloat16)
            return carry

        lax.fori_loop(q * 2, q * 2 + 2, body, 0)

    def t_wait(j, q):
        h, part = j // X, j % X
        if (part, q) in ((1, 0), (2, 1)):
            arrived(relay.at[h, :, side(q)], t_recv.at[h, 0, q])
        if part == 3:
            arrived(near.at[h, 0, :, side(q)], t_recv.at[h, 1, q])
            arrived(near.at[h, 1, :, side(q)], t_recv.at[h, 2, q])

    def t_put(j, q):
        h, part = j // X, j % X
        if part == 3:
            g_first(h, q)
            return
        way = (q, 0, 1)[part]
        dst = relay.at[h, :, side(q)] if part == 0 else near.at[h, way, :, side(q)]
        put(t_buf.at[h, part, :, side(q)], dst, t_send.at[h, part, q], t_recv.at[h, part, q], on_x(sign[way]))

    def term(j, q):
        t_wait(j, q)
        multiply(j, q)
        t_put(j, q)

    def own_rows():
        return jnp.concatenate([g_buf[g_rows(0, x), :], g_buf[g_rows(1, x), :]], axis=0)

    def keep(which, cols, value):
        value = value.astype(jnp.bfloat16)
        o_buf[which, 0, :, cols] = value[:PIECE]
        o_buf[which, 1, :, cols] = value[PIECE:]

    outs = (left_ref, right_ref, upd_ref)
    kept = []
    inverse = 1.0 / BLOCK

    def ship(which, q):
        put(o_buf.at[which, other, :, side(q)], outs[which].at[zl, :, side(q)],
            o_send.at[which, q], o_recv.at[which, q], partner)
        copy = pltpu.make_async_copy(
            o_buf.at[which, zl, :, side(q)], outs[which].at[zl, :, side(q)], local_sem.at[4 + which * 2 + q])
        copy.start()
        kept.append(copy)

    def over_tiles(first, last, tile):
        def body(n, carry):
            tile(columns(n))
            return carry
        lax.fori_loop(first, last, body, 0)

    def left_part(h):
        def tile(cols):
            keep(0, cols, inverse * lax.dot_general(
                own_rows(), g_buf[cols, :], (((1,), (1,)), ((), ())),
                preferred_element_type=jnp.float32))
        over_tiles(h * 2, h * 2 + 2, tile)
        ship(0, h)

    def turn_own(h):
        rows = pl.ds(h * HALF, HALF)
        for i in (0, 1):
            gt_buf[pl.ds(i * PIECE, PIECE), rows] = g_buf[rows, g_rows(i, x)].T

    def right_part(h):
        rows = pl.ds(h * HALF, HALF)
        turn_own(h)

        def tile(cols):
            value = inverse * jnp.dot(gt_buf[:, rows], g_buf[rows, cols], preferred_element_type=jnp.float32)
            if h == 0:
                right_acc[:, cols] = value
            else:
                keep(1, cols, right_acc[:, cols] + value)
        for q in (0, 1):
            over_tiles(q * 2, q * 2 + 2, tile)
            if h == 1:
                ship(1, q)

    def lift_part(h):
        rows = pl.ds(h * HALF, HALF)

        def tile(cols):
            roots = l_buf[:, :, rows].reshape(2 * PIECE, HALF)
            value = jnp.dot(roots, g_buf[rows, cols], preferred_element_type=jnp.float32)
            if h == 0:
                lift_acc[:, cols] = value
            else:
                lift_buf[:, cols] = (lift_acc[:, cols] + value).astype(jnp.bfloat16)
        over_tiles(0, 4, tile)

    def update_part():
        def tile(cols):
            keep(2, cols, jnp.dot(
                lift_buf[...], r_buf[:, :, :, cols].reshape(BLOCK, TILE),
                preferred_element_type=jnp.float32))
        for q in (0, 1):
            over_tiles(q * 2, q * 2 + 2, tile)
            ship(2, q)

    put(c_ref.at[:, :, pl.ds(scaled(other, BLOCK), BLOCK)], c_chunk(zl, f),
        swap_send.at[0], swap_recv.at[0], partner)
    a_first(0)
    put(rr_ref.at[other], r_chunk(zl, x), swap_send.at[1], swap_recv.at[1], partner)
    r_first(rr_ref.at[zl], zl)
    c_first(c_ref.at[:, :, pl.ds(scaled(zl, BLOCK), BLOCK)], zl)
    arrived(c_chunk(other, f), swap_recv.at[0])
    c_first(c_chunk(other, f), other)
    local[0].wait()
    a_event(0)
    a_strips(0)
    for j in range(4):
        z_first(j)
    arrived(r_chunk(other, x), swap_recv.at[1])
    r_first(r_chunk(other, x), other)
    for step in (1, 2, 3, 4):
        c_event(step)
        for j in range(4):
            z_event(j, step)
        if step == 2:
            a_first(1)
            put(lr_ref.at[other], l_buf.at[zl], swap_send.at[2], swap_recv.at[2], partner)
            r_event(1)
    local[1].wait()
    turn(0)
    c_rest()
    term(0, 0)
    term(0, 1)
    turn(1)
    term(1, 1)
    turn(2)
    term(2, 0)
    a_event(1)
    a_strips(1)
    z_first(4)
    z_first(5)
    term(1, 0)
    term(2, 1)
    turn(3)
    z_event(4, 1)
    z_first(6)
    z_event(4, 2)
    z_event(5, 1)
    z_first(7)
    term(3, 0)
    z_event(4, 3)
    term(3, 1)
    z_event(5, 2)
    z_event(6, 1)
    z_event(4, 4)
    turn(4)
    z_event(5, 3)
    z_event(6, 2)
    z_event(7, 1)
    term(4, 0)
    term(4, 1)
    z_event(5, 4)
    z_event(6, 3)
    z_event(7, 2)
    turn(5)
    g_event(0, 1)
    term(5, 1)
    z_event(6, 4)
    z_event(7, 3)
    turn(6)
    term(6, 0)
    term(5, 0)
    term(6, 1)
    z_event(7, 4)
    turn(7)
    term(7, 0)
    term(7, 1)
    g_event(0, 2)
    left_part(0)
    right_part(0)
    local[2].wait()
    arrived(l_buf.at[other], swap_recv.at[2])
    lift_part(0)
    g_event(1, 1)
    local[3].wait()
    r_event(2)
    g_event(1, 2)
    right_part(1)
    lift_part(1)
    update_part()
    left_part(1)

    a_drain(0)
    a_drain(1)
    for copy in started:
        copy.wait_send()
    for copy in kept:
        copy.wait()
    for which in range(3):
        for q in (0, 1):
            arrived(outs[which].at[other, :, side(q)], o_recv.at[which, q])


def on_device(activations, cotangent, left_root, right_root):
    tokens = cotangent.shape[0]
    factor = float(tokens * lax.axis_size("dp") * lax.axis_size("fsdp")) ** (-0.5)
    bf16 = jnp.bfloat16
    dma = pltpu.SemaphoreType.DMA
    anywhere = pl.BlockSpec(memory_space=pltpu.HBM)
    piece = jax.ShapeDtypeStruct((2, PIECE, BLOCK), bf16)
    left, right, update = pl.pallas_call(
        functools.partial(kernel, factor),
        out_shape=(piece, piece, piece),
        in_specs=[anywhere] * 4,
        out_specs=(anywhere,) * 3,
        scratch_shapes=[
            pltpu.VMEM((SLOT, BLOCK), bf16),
            pltpu.VMEM((2 * X, Z, SLOT, PIECE), bf16),
            pltpu.VMEM((Z, SLOT, BLOCK), bf16),
            pltpu.VMEM((BLOCK, BLOCK), bf16),
            pltpu.VMEM((2, X, PIECE, BLOCK), bf16),
            pltpu.VMEM((2, PIECE, BLOCK), bf16),
            pltpu.VMEM((X, PIECE, Z * SLOT), bf16),
            pltpu.VMEM((2, 3, PIECE, BLOCK), bf16),
            pltpu.VMEM((2, PIECE, BLOCK), bf16),
            pltpu.VMEM((2, 2, PIECE, BLOCK), bf16),
            pltpu.VMEM((2 * PIECE, BLOCK), bf16),
            pltpu.VMEM((2 * PIECE, BLOCK), bf16),
            pltpu.VMEM((2 * PIECE, BLOCK), jnp.float32),
            pltpu.VMEM((2 * PIECE, BLOCK), jnp.float32),
            pltpu.VMEM((3, 2, PIECE, BLOCK), bf16),
            dma((10,)), dma((3,)), dma((3,)),
            dma((2, F)), dma((2, F)),
            dma((2, 2, 5)), dma((2, 2, 5)), dma((2, 2, 5)), dma((2, 2, 5)),
            dma((2, 8, 5)), dma((2, 8, 5)),
            dma((2, 3, 2)), dma((2, 3, 2)),
            dma((2, 2, 2, 3)), dma((2, 2, 2, 3)),
            dma((2, 2, 3)), dma((2, 2, 3)),
            dma((3, 2)), dma((3, 2)),
        ],
        compiler_params=pltpu.CompilerParams(
            collective_id=0, has_side_effects=True, vmem_limit_bytes=62 * 1024 * 1024
        ),
        cost_estimate=pl.CostEstimate(
            flops=6 * 2**30, bytes_accessed=8 * 2**20, transcendentals=0),
    )(
        activations,
        cotangent.reshape(T, ROWS, 2 * BLOCK),
        left_root.reshape(2, PIECE, BLOCK),
        right_root.reshape(2, PIECE, BLOCK),
    )
    shape = left_root.shape
    return (
        left.reshape(shape).astype(jnp.float32),
        right.reshape(shape).astype(jnp.float32),
        update.reshape(shape),
    )


def solution(mesh):
    return jax.shard_map(
        on_device,
        mesh=mesh,
        in_specs=(
            P(("dp", "fsdp", "tensor"), None),
            P(("dp", "fsdp"), "tensor"),
            P("fsdp", "tensor", "dp", None),
            P("fsdp", "tensor", "dp", None),
        ),
        out_specs=(
            P("fsdp", "tensor", "dp", None),
            P("fsdp", "tensor", "dp", None),
            P("fsdp", "tensor", "dp", None),
        ),
        check_vma=False,
    )
```

```python
import functools

import jax
import jax.numpy as jnp
from jax import lax
from jax.experimental import pallas as pl
from jax.experimental.pallas import tpu as pltpu
from jax.sharding import PartitionSpec as P

MESH = pl.DeviceIdType.MESH
X, Y, Z, CORES = 4, 8, 8, 2
F = Y * CORES
T = Z // 2
PIECE = 128
BLOCK = 1024
HALF = BLOCK // 2
ROWS = 16
SLOT = F * ROWS
TILE = 256


def mod(value, size):
    return lax.rem(value + 2 * size, size)


def scaled(index, size):
    return pl.multiple_of(index * size, size)


def kernel(
    factor,
    a_ref, c_ref, lr_ref, rr_ref,
    out_ref,
    stage, a_buf, c_buf, g_buf, r_buf, l_buf, at_buf, t_buf, relay, near, gt_buf, lift_buf,
    right_acc, lift_acc, o_buf,
    local_sem, swap_send, swap_recv,
    a_send, a_recv, c_send, c_recv, sib_send, sib_recv,
    z_send, z_recv, t_send, t_recv, g_send, g_recv, r_send, r_recv, o_send, o_recv,
):
    m = lax.axis_index("dp")
    f = lax.axis_index("fsdp")
    t = lax.axis_index("tensor")
    zl, x = lax.div(m, X), lax.rem(m, X)
    y, core = lax.div(f, CORES), lax.rem(f, CORES)
    z = 2 * t + zl
    other = 1 - zl

    def on_x(step):
        return (zl * X + mod(x + step, X), f, t)

    def on_y(step):
        return (m, mod(y + step, Y) * CORES + core, t)

    def on_z(step):
        there = mod(z + step, Z)
        return (lax.rem(there, 2) * X + x, f, lax.div(there, 2))

    def slot_of(there):
        return lax.rem(there, 2) * T + lax.div(there, 2)

    sibling = (m, y * CORES + 1 - core, t)
    partner = (other * X + x, f, t)
    sign = (1, -1)
    slot = slot_of(z)
    my_rows = scaled(f, ROWS)

    started = []

    def put(src, dst, send, recv, device):
        copy = pltpu.make_async_remote_copy(
            src_ref=src, dst_ref=dst, send_sem=send, recv_sem=recv,
            device_id=device, device_id_type=MESH,
        )
        copy.start()
        started.append(copy)

    def arrived(dst, recv):
        pltpu.make_async_remote_copy(
            src_ref=dst, dst_ref=dst, send_sem=recv, recv_sem=recv,
            device_id=sibling, device_id_type=MESH,
        ).wait_recv()

    barrier = pltpu.get_barrier_semaphore()

    def greet(d, carry):
        pl.semaphore_signal(barrier, inc=1, device_id=(m, mod(f + d, F), t), device_id_type=MESH)
        return carry

    for device in (on_z(1), on_z(-1), on_x(1), on_x(-1)):
        pl.semaphore_signal(barrier, inc=1, device_id=device, device_id_type=MESH)
    lax.fori_loop(1, F, greet, 0)

    local = [
        pltpu.make_async_copy(
            a_ref.at[:, pl.ds(scaled(f, BLOCK), BLOCK)],
            stage.at[pl.ds(my_rows, ROWS), :], local_sem.at[0]),
        pltpu.make_async_copy(
            c_ref.at[:, :, pl.ds(scaled(zl, BLOCK), BLOCK)],
            c_buf.at[pl.ds(zl * T, T), pl.ds(my_rows, ROWS), :], local_sem.at[1]),
        pltpu.make_async_copy(lr_ref.at[zl], l_buf.at[zl], local_sem.at[2]),
        pltpu.make_async_copy(rr_ref.at[zl], r_buf.at[zl, x], local_sem.at[3]),
    ]
    for copy in local:
        copy.start()
    pl.semaphore_wait(barrier, F - 1 + 4)

    def a_copy(part, d):
        to = mod(f + d, F)
        start = pl.multiple_of(to * BLOCK + part * HALF, HALF)
        return pltpu.make_async_remote_copy(
            src_ref=a_ref.at[:, pl.ds(start, HALF)],
            dst_ref=stage.at[pl.ds(my_rows, ROWS), pl.ds(part * HALF, HALF)],
            send_sem=a_send.at[part, d], recv_sem=a_recv.at[part, d],
            device_id=(m, to, t), device_id_type=MESH)

    def a_first(part):
        def body(d, carry):
            a_copy(part, d).start()
            return carry
        lax.fori_loop(1, F, body, 0)

    def a_event(part):
        def body(d, carry):
            rows = pl.ds(scaled(mod(f - d, F), ROWS), ROWS)
            arrived(stage.at[rows, pl.ds(part * HALF, HALF)], a_recv.at[part, d])
            return carry
        lax.fori_loop(1, F, body, 0)

    def a_drain(part):
        def body(d, carry):
            a_copy(part, d).wait_send()
            return carry
        lax.fori_loop(1, F, body, 0)

    def a_strips(part):
        for i in range(part * X, part * X + X):
            a_buf[i, slot] = stage[:, i * PIECE:(i + 1) * PIECE]

    def c_chunk(half, owner):
        return c_buf.at[pl.ds(half * T, T), pl.ds(scaled(owner, ROWS), ROWS), :]

    def c_share(src, half, owner, way, step):
        put(src, c_chunk(half, owner), sib_send.at[half, way, step], sib_recv.at[half, way, step], sibling)

    def c_first(src, half):
        for way in (0, 1):
            put(src, c_chunk(half, f), c_send.at[way, half, 0], c_recv.at[way, half, 1], on_y(sign[way]))
        c_share(src, half, f, 0, 0)

    def c_event(step, half):
        for way in (0, 1):
            if step == Y // 2 and way != half:
                continue
            owner = mod(y - sign[way] * step, Y) * CORES + core
            chunk = c_chunk(half, owner)
            arrived(chunk, c_recv.at[way, half, step])
            if step < Y // 2 - 1 or (step == Y // 2 - 1 and way == half):
                put(chunk, chunk, c_send.at[way, half, step], c_recv.at[way, half, step + 1],
                    on_y(sign[way]))
            c_share(chunk, half, owner, way, step)

    def c_rest():
        for step in range(Y // 2 + 1):
            for half in (0, 1):
                for way in (0, 1):
                    if (step == Y // 2 and way != half) or (step == 0 and way == 1):
                        continue
                    owner = mod(y - sign[way] * step, Y) * CORES + 1 - core
                    arrived(c_chunk(half, owner), sib_recv.at[half, way, step])

    target = (mod(x + 2, X), mod(x + 1, X), mod(x - 1, X), x)

    def strip(j):
        return (j // X) * X + target[j % X]

    def z_put(j, way, step, owner):
        ref = a_buf.at[strip(j), owner]
        put(ref, ref, z_send.at[way, j, step], z_recv.at[way, j, step + 1], on_z(sign[way]))

    def z_first(j):
        for way in (0, 1):
            z_put(j, way, 0, slot)

    def z_event(j, step):
        for way in (0, 1):
            if step == Z // 2 and way != j % 2:
                continue
            owner = slot_of(mod(z - sign[way] * step, Z))
            arrived(a_buf.at[strip(j), owner], z_recv.at[way, j, step])
            if step < Z // 2 - 1 or (step == Z // 2 - 1 and way == j % 2):
                z_put(j, way, step, owner)

    def x_first(src_of, dst_of, send, recv, half):
        for way in (0, 1):
            put(src_of, dst_of, send.at[way, half, 0], recv.at[way, half, 1], on_x(sign[way]))

    def x_ring(ref_of, send, recv, step):
        for turned in (0, 1):
            for way in (0, 1):
                half = (way + turned) % 2
                if step == X // 2 and way != half:
                    continue
                ref = ref_of(half, mod(x - sign[way] * step, X))
                arrived(ref, recv.at[way, half, step])
                if step < X // 2 - 1 or (step == X // 2 - 1 and way == half):
                    put(ref, ref, send.at[way, half, step], recv.at[way, half, step + 1], on_x(sign[way]))

    def r_chunk(half, owner):
        return r_buf.at[half, owner]

    def r_first(src, half):
        x_first(src, r_chunk(half, x), r_send, r_recv, half)

    def r_event(step):
        x_ring(r_chunk, r_send, r_recv, step)

    def g_rows(h, owner):
        return pl.ds(pl.multiple_of((h * X + owner) * PIECE, PIECE), PIECE)

    def side(q):
        return pl.ds(q * HALF, HALF)

    def g_chunk(h):
        return lambda q, owner: g_buf.at[g_rows(h, owner), side(q)]

    def g_first(h):
        for q in (0, 1):
            for way in (0, 1):
                half = (way + q) % 2
                ref = g_chunk(h)(half, x)
                put(ref, ref, g_send.at[h, way, half, 0], g_recv.at[h, way, half, 1], on_x(sign[way]))

    def g_event(h, step):
        x_ring(g_chunk(h), g_send.at[h], g_recv.at[h], step)

    def columns(n):
        return pl.ds(pl.multiple_of(n * TILE, TILE), TILE)

    def turn(j):
        for k in range(Z):
            at_buf[j % X, :, pl.ds(k * SLOT, SLOT)] = a_buf[strip(j), k].T

    def multiply(j, q):
        h, part = j // X, j % X

        def body(n, carry):
            cols = columns(n)
            value = jnp.dot(
                at_buf[part], c_buf[:, :, cols].reshape(Z * SLOT, TILE),
                preferred_element_type=jnp.float32,
            ) * factor
            if (part, q) in ((1, 0), (2, 1)):
                value = value + relay[h, :, cols].astype(jnp.float32)
            if part == 3:
                value = value + near[h, 0, :, cols].astype(jnp.float32) + near[h, 1, :, cols].astype(jnp.float32)
                g_buf[g_rows(h, x), cols] = value.astype(jnp.bfloat16)
            else:
                t_buf[h, part, :, cols] = value.astype(jnp.bfloat16)
            return carry

        lax.fori_loop(q * 2, q * 2 + 2, body, 0)

    def t_wait(j, q):
        h, part = j // X, j % X
        if (part, q) in ((1, 0), (2, 1)):
            arrived(relay.at[h, :, side(q)], t_recv.at[h, 0, q])
        if part == 3:
            arrived(near.at[h, 0, :, side(q)], t_recv.at[h, 1, q])
            arrived(near.at[h, 1, :, side(q)], t_recv.at[h, 2, q])

    def t_put(j, q):
        h, part = j // X, j % X
        if part == 3:
            if q == 1:
                g_first(h)
            return
        way = (q, 0, 1)[part]
        dst = relay.at[h, :, side(q)] if part == 0 else near.at[h, way, :, side(q)]
        put(t_buf.at[h, part, :, side(q)], dst, t_send.at[h, part, q], t_recv.at[h, part, q], on_x(sign[way]))

    def term(j, q):
        t_wait(j, q)
        multiply(j, q)
        t_put(j, q)

    def own_rows():
        return jnp.concatenate([g_buf[g_rows(0, x), :], g_buf[g_rows(1, x), :]], axis=0)

    def keep(which, cols, value):
        value = value.astype(jnp.bfloat16)
        o_buf[which, 0, :, cols] = value[:PIECE]
        o_buf[which, 1, :, cols] = value[PIECE:]

    kept = []
    inverse = 1.0 / BLOCK

    def ship(which, cols, i):
        put(o_buf.at[which, other, :, cols], out_ref.at[which, zl, :, cols],
            o_send.at[which, i], o_recv.at[which, i], partner)
        copy = pltpu.make_async_copy(
            o_buf.at[which, zl, :, cols], out_ref.at[which, zl, :, cols], local_sem.at[4 + which * 5 + i])
        copy.start()
        kept.append(copy)

    def over_tiles(first, last, tile):
        def body(n, carry):
            tile(columns(n))
            return carry
        lax.fori_loop(first, last, body, 0)

    def left_tile(cols):
        keep(0, cols, inverse * lax.dot_general(
            own_rows(), g_buf[cols, :], (((1,), (1,)), ((), ())),
            preferred_element_type=jnp.float32))

    def left_part():
        over_tiles(0, 2, left_tile)
        ship(0, side(0), 0)

    def left_piece(i):
        cols = g_rows(1, target[i])
        left_tile(cols)
        ship(0, cols, 1 + i)

    def turn_own(h):
        rows = pl.ds(h * HALF, HALF)
        for i in (0, 1):
            gt_buf[pl.ds(i * PIECE, PIECE), rows] = g_buf[rows, g_rows(i, x)].T

    def right_part(h):
        rows = pl.ds(h * HALF, HALF)
        turn_own(h)

        def tile(cols):
            value = inverse * jnp.dot(gt_buf[:, rows], g_buf[rows, cols], preferred_element_type=jnp.float32)
            if h == 0:
                right_acc[:, cols] = value
            else:
                keep(1, cols, right_acc[:, cols] + value)
        for q in (0, 1):
            over_tiles(q * 2, q * 2 + 2, tile)
            if h == 1:
                ship(1, side(q), q)

    def lift_part(h):
        rows = pl.ds(h * HALF, HALF)

        def tile(cols):
            roots = l_buf[:, :, rows].reshape(2 * PIECE, HALF)
            value = jnp.dot(roots, g_buf[rows, cols], preferred_element_type=jnp.float32)
            if h == 0:
                lift_acc[:, cols] = value
            else:
                lift_buf[:, cols] = (lift_acc[:, cols] + value).astype(jnp.bfloat16)
        over_tiles(0, 4, tile)

    def update_part():
        def tile(cols):
            keep(2, cols, jnp.dot(
                lift_buf[...], r_buf[:, :, :, cols].reshape(BLOCK, TILE),
                preferred_element_type=jnp.float32))
        for q in (0, 1):
            over_tiles(q * 2, q * 2 + 2, tile)
            ship(2, side(q), q)

    put(c_ref.at[:, :, pl.ds(scaled(other, BLOCK), BLOCK)], c_chunk(zl, f),
        swap_send.at[0], swap_recv.at[0], partner)
    a_first(0)
    put(rr_ref.at[other], r_chunk(zl, x), swap_send.at[1], swap_recv.at[1], partner)
    r_first(rr_ref.at[zl], zl)
    arrived(c_chunk(other, f), swap_recv.at[0])
    c_first(c_ref.at[:, :, pl.ds(scaled(zl, BLOCK), BLOCK)], zl)
    c_first(c_chunk(other, f), other)
    local[0].wait()
    a_event(0)
    a_strips(0)
    for j in range(4):
        z_first(j)
    arrived(r_chunk(other, x), swap_recv.at[1])
    r_first(r_chunk(other, x), other)
    c_event(1, 0)
    c_event(1, 1)
    z_event(0, 1)
    z_event(1, 1)
    c_event(2, 0)
    z_event(2, 1)
    z_event(3, 1)
    c_event(2, 1)
    z_event(0, 2)
    z_event(1, 2)
    r_event(1)
    c_event(3, 0)
    a_first(1)
    z_event(2, 2)
    z_event(3, 2)
    c_event(3, 1)
    z_event(0, 3)
    z_event(1, 3)
    put(lr_ref.at[other], l_buf.at[zl], swap_send.at[2], swap_recv.at[2], partner)
    z_event(2, 3)
    z_event(3, 3)
    a_event(1)
    a_strips(1)
    z_first(4)
    z_first(5)
    z_first(6)
    local[1].wait()
    c_event(4, 0)
    c_event(4, 1)
    z_event(0, 4)
    turn(0)
    z_event(1, 4)
    turn(1)
    c_rest()
    term(0, 0)
    term(0, 1)
    z_event(4, 1)
    z_event(5, 1)
    z_first(7)
    term(1, 1)
    z_event(2, 4)
    turn(2)
    term(2, 0)
    z_event(3, 4)
    turn(3)
    z_event(6, 1)
    z_event(4, 2)
    z_event(5, 2)
    term(1, 0)
    z_event(7, 1)
    term(2, 1)
    z_event(4, 3)
    z_event(6, 2)
    z_event(5, 3)
    term(3, 0)
    term(3, 1)
    z_event(7, 2)
    z_event(4, 4)
    turn(4)
    term(4, 0)
    term(4, 1)
    z_event(5, 4)
    turn(5)
    term(5, 1)
    z_event(6, 3)
    z_event(7, 3)
    z_event(6, 4)
    turn(6)
    term(6, 0)
    g_event(0, 1)
    term(5, 0)
    term(6, 1)
    z_event(7, 4)
    turn(7)
    term(7, 0)
    term(7, 1)
    g_event(0, 2)
    left_part()
    right_part(0)
    local[2].wait()
    arrived(l_buf.at[other], swap_recv.at[2])
    lift_part(0)
    left_piece(3)
    g_event(1, 1)
    left_piece(2)
    left_piece(1)
    local[3].wait()
    r_event(2)
    g_event(1, 2)
    right_part(1)
    lift_part(1)
    update_part()
    left_piece(0)

    a_drain(0)
    a_drain(1)
    for copy in started:
        copy.wait_send()
    for copy in kept:
        copy.wait()
    for which in (1, 2):
        for q in (0, 1):
            arrived(out_ref.at[which, other, :, side(q)], o_recv.at[which, q])
    arrived(out_ref.at[0, other, :, side(0)], o_recv.at[0, 0])
    for i in range(X):
        arrived(out_ref.at[0, other, :, g_rows(1, target[i])], o_recv.at[0, 1 + i])


def on_device(activations, cotangent, left_root, right_root):
    tokens = cotangent.shape[0]
    factor = float(tokens * lax.axis_size("dp") * lax.axis_size("fsdp")) ** (-0.5)
    bf16 = jnp.bfloat16
    dma = pltpu.SemaphoreType.DMA
    anywhere = pl.BlockSpec(memory_space=pltpu.HBM)
    out = pl.pallas_call(
        functools.partial(kernel, factor),
        out_shape=jax.ShapeDtypeStruct((3, 2, PIECE, BLOCK), bf16),
        in_specs=[anywhere] * 4,
        out_specs=anywhere,
        scratch_shapes=[
            pltpu.VMEM((SLOT, BLOCK), bf16),
            pltpu.VMEM((2 * X, Z, SLOT, PIECE), bf16),
            pltpu.VMEM((Z, SLOT, BLOCK), bf16),
            pltpu.VMEM((BLOCK, BLOCK), bf16),
            pltpu.VMEM((2, X, PIECE, BLOCK), bf16),
            pltpu.VMEM((2, PIECE, BLOCK), bf16),
            pltpu.VMEM((X, PIECE, Z * SLOT), bf16),
            pltpu.VMEM((2, 3, PIECE, BLOCK), bf16),
            pltpu.VMEM((2, PIECE, BLOCK), bf16),
            pltpu.VMEM((2, 2, PIECE, BLOCK), bf16),
            pltpu.VMEM((2 * PIECE, BLOCK), bf16),
            pltpu.VMEM((2 * PIECE, BLOCK), bf16),
            pltpu.VMEM((2 * PIECE, BLOCK), jnp.float32),
            pltpu.VMEM((2 * PIECE, BLOCK), jnp.float32),
            pltpu.VMEM((3, 2, PIECE, BLOCK), bf16),
            dma((20,)), dma((3,)), dma((3,)),
            dma((2, F)), dma((2, F)),
            dma((2, 2, 5)), dma((2, 2, 5)), dma((2, 2, 5)), dma((2, 2, 5)),
            dma((2, 8, 5)), dma((2, 8, 5)),
            dma((2, 3, 2)), dma((2, 3, 2)),
            dma((2, 2, 2, 3)), dma((2, 2, 2, 3)),
            dma((2, 2, 3)), dma((2, 2, 3)),
            dma((3, 5)), dma((3, 5)),
        ],
        compiler_params=pltpu.CompilerParams(
            collective_id=0, has_side_effects=True, vmem_limit_bytes=62 * 1024 * 1024
        ),
        cost_estimate=pl.CostEstimate(
            flops=6 * 2**30, bytes_accessed=8 * 2**20, transcendentals=0),
    )(
        activations,
        cotangent.reshape(T, ROWS, 2 * BLOCK),
        left_root.reshape(2, PIECE, BLOCK),
        right_root.reshape(2, PIECE, BLOCK),
    )
    shape = left_root.shape
    return (
        out[0].reshape(shape).astype(jnp.float32),
        out[1].reshape(shape).astype(jnp.float32),
        out[2].reshape(shape),
    )


def solution(mesh):
    return jax.shard_map(
        on_device,
        mesh=mesh,
        in_specs=(
            P(("dp", "fsdp", "tensor"), None),
            P(("dp", "fsdp"), "tensor"),
            P("fsdp", "tensor", "dp", None),
            P("fsdp", "tensor", "dp", None),
        ),
        out_specs=(
            P("fsdp", "tensor", "dp", None),
            P("fsdp", "tensor", "dp", None),
            P("fsdp", "tensor", "dp", None),
        ),
        check_vma=False,
    )
```

```python
import functools

import jax
import jax.numpy as jnp
from jax import lax
from jax.experimental import pallas as pl
from jax.experimental.pallas import tpu as pltpu
from jax.sharding import PartitionSpec as P

MESH = pl.DeviceIdType.MESH
X, Y, Z, CORES = 4, 8, 8, 2
F = Y * CORES
T = Z // 2
PIECE = 128
BLOCK = 1024
HALF = BLOCK // 2
ROWS = 16
SLOT = F * ROWS
TILE = 256


def mod(value, size):
    return lax.rem(value + 2 * size, size)


def scaled(index, size):
    return pl.multiple_of(index * size, size)


def kernel(
    factor,
    a_ref, c_ref, lr_ref, rr_ref,
    out_ref,
    stage, a_buf, c_buf, g_buf, r_buf, l_buf, at_buf, t_buf, relay, near, gt_buf, lift_buf,
    right_acc, lift_acc, o_buf,
    local_sem, swap_send, swap_recv,
    a_send, a_recv, c_send, c_recv, sib_send, sib_recv,
    z_send, z_recv, t_send, t_recv, g_send, g_recv, r_send, r_recv, o_send, o_recv,
):
    m = lax.axis_index("dp")
    f = lax.axis_index("fsdp")
    t = lax.axis_index("tensor")
    zl, x = lax.div(m, X), lax.rem(m, X)
    y, core = lax.div(f, CORES), lax.rem(f, CORES)
    z = 2 * t + zl
    other = 1 - zl

    def on_x(step):
        return (zl * X + mod(x + step, X), f, t)

    def on_y(step):
        return (m, mod(y + step, Y) * CORES + core, t)

    def on_z(step):
        there = mod(z + step, Z)
        return (lax.rem(there, 2) * X + x, f, lax.div(there, 2))

    def slot_of(there):
        return lax.rem(there, 2) * T + lax.div(there, 2)

    sibling = (m, y * CORES + 1 - core, t)
    partner = (other * X + x, f, t)
    sign = (1, -1)
    slot = slot_of(z)
    my_rows = scaled(f, ROWS)

    started = []

    def put(src, dst, send, recv, device):
        copy = pltpu.make_async_remote_copy(
            src_ref=src, dst_ref=dst, send_sem=send, recv_sem=recv,
            device_id=device, device_id_type=MESH,
        )
        copy.start()
        started.append(copy)

    def arrived(dst, recv):
        pltpu.make_async_remote_copy(
            src_ref=dst, dst_ref=dst, send_sem=recv, recv_sem=recv,
            device_id=sibling, device_id_type=MESH,
        ).wait_recv()

    barrier = pltpu.get_barrier_semaphore()

    def greet(d, carry):
        pl.semaphore_signal(barrier, inc=1, device_id=(m, mod(f + d, F), t), device_id_type=MESH)
        return carry

    for device in (on_z(1), on_z(-1), on_x(1), on_x(-1)):
        pl.semaphore_signal(barrier, inc=1, device_id=device, device_id_type=MESH)
    lax.fori_loop(1, F, greet, 0)

    local = [
        pltpu.make_async_copy(
            a_ref.at[:, pl.ds(scaled(f, BLOCK), BLOCK)],
            stage.at[pl.ds(my_rows, ROWS), :], local_sem.at[0]),
        pltpu.make_async_copy(
            c_ref.at[:, :, pl.ds(scaled(zl, BLOCK), BLOCK)],
            c_buf.at[pl.ds(zl * T, T), pl.ds(my_rows, ROWS), :], local_sem.at[1]),
        pltpu.make_async_copy(lr_ref.at[zl], l_buf.at[zl], local_sem.at[2]),
        pltpu.make_async_copy(rr_ref.at[zl], r_buf.at[zl, x], local_sem.at[3]),
    ]
    for copy in local:
        copy.start()
    pl.semaphore_wait(barrier, F - 1 + 4)

    def a_copy(part, d):
        to = mod(f + d, F)
        start = pl.multiple_of(to * BLOCK + part * HALF, HALF)
        return pltpu.make_async_remote_copy(
            src_ref=a_ref.at[:, pl.ds(start, HALF)],
            dst_ref=stage.at[pl.ds(my_rows, ROWS), pl.ds(part * HALF, HALF)],
            send_sem=a_send.at[part, d], recv_sem=a_recv.at[part, d],
            device_id=(m, to, t), device_id_type=MESH)

    def a_first(part):
        def body(d, carry):
            a_copy(part, d).start()
            return carry
        lax.fori_loop(1, F, body, 0)

    def a_event(part):
        def body(d, carry):
            rows = pl.ds(scaled(mod(f - d, F), ROWS), ROWS)
            arrived(stage.at[rows, pl.ds(part * HALF, HALF)], a_recv.at[part, d])
            return carry
        lax.fori_loop(1, F, body, 0)

    def a_drain(part):
        def body(d, carry):
            a_copy(part, d).wait_send()
            return carry
        lax.fori_loop(1, F, body, 0)

    def a_strips(part):
        for i in range(part * X, part * X + X):
            a_buf[i, slot] = stage[:, i * PIECE:(i + 1) * PIECE]

    def c_chunk(half, owner):
        return c_buf.at[pl.ds(half * T, T), pl.ds(scaled(owner, ROWS), ROWS), :]

    def c_share(src, half, owner, way, step):
        put(src, c_chunk(half, owner), sib_send.at[half, way, step], sib_recv.at[half, way, step], sibling)

    def c_first(src, half):
        for way in (0, 1):
            put(src, c_chunk(half, f), c_send.at[way, half, 0], c_recv.at[way, half, 1], on_y(sign[way]))
        c_share(src, half, f, 0, 0)

    def c_event(step, half):
        for way in (0, 1):
            if step == Y // 2 and way != half:
                continue
            owner = mod(y - sign[way] * step, Y) * CORES + core
            chunk = c_chunk(half, owner)
            arrived(chunk, c_recv.at[way, half, step])
            if step < Y // 2 - 1 or (step == Y // 2 - 1 and way == half):
                put(chunk, chunk, c_send.at[way, half, step], c_recv.at[way, half, step + 1],
                    on_y(sign[way]))
            c_share(chunk, half, owner, way, step)

    def c_rest():
        for step in range(Y // 2 + 1):
            for half in (0, 1):
                for way in (0, 1):
                    if (step == Y // 2 and way != half) or (step == 0 and way == 1):
                        continue
                    owner = mod(y - sign[way] * step, Y) * CORES + 1 - core
                    arrived(c_chunk(half, owner), sib_recv.at[half, way, step])

    target = (mod(x + 2, X), mod(x + 1, X), mod(x - 1, X), x)

    def strip(j):
        return (j // X) * X + target[j % X]

    def z_put(j, way, step, owner):
        ref = a_buf.at[strip(j), owner]
        put(ref, ref, z_send.at[way, j, step], z_recv.at[way, j, step + 1], on_z(sign[way]))

    def z_first(j):
        for way in (0, 1):
            z_put(j, way, 0, slot)

    def z_event(j, step):
        for way in (0, 1):
            if step == Z // 2 and way != j % 2:
                continue
            owner = slot_of(mod(z - sign[way] * step, Z))
            arrived(a_buf.at[strip(j), owner], z_recv.at[way, j, step])
            if step < Z // 2 - 1 or (step == Z // 2 - 1 and way == j % 2):
                z_put(j, way, step, owner)

    def x_first(src_of, dst_of, send, recv, half):
        for way in (0, 1):
            put(src_of, dst_of, send.at[way, half, 0], recv.at[way, half, 1], on_x(sign[way]))

    def x_ring(ref_of, send, recv, step):
        for turned in (0, 1):
            for way in (0, 1):
                half = (way + turned) % 2
                if step == X // 2 and way != half:
                    continue
                ref = ref_of(half, mod(x - sign[way] * step, X))
                arrived(ref, recv.at[way, half, step])
                if step < X // 2 - 1 or (step == X // 2 - 1 and way == half):
                    put(ref, ref, send.at[way, half, step], recv.at[way, half, step + 1], on_x(sign[way]))

    def r_chunk(half, owner):
        return r_buf.at[half, owner]

    def r_first(src, half):
        x_first(src, r_chunk(half, x), r_send, r_recv, half)

    def r_event(step):
        x_ring(r_chunk, r_send, r_recv, step)

    def g_rows(h, owner):
        return pl.ds(pl.multiple_of((h * X + owner) * PIECE, PIECE), PIECE)

    def side(q):
        return pl.ds(q * HALF, HALF)

    def g_chunk(h):
        return lambda q, owner: g_buf.at[g_rows(h, owner), side(q)]

    def g_first(h):
        for q in (0, 1):
            for way in (0, 1):
                half = (way + q) % 2
                ref = g_chunk(h)(half, x)
                put(ref, ref, g_send.at[h, way, half, 0], g_recv.at[h, way, half, 1], on_x(sign[way]))

    def g_event(h, step):
        x_ring(g_chunk(h), g_send.at[h], g_recv.at[h], step)

    def columns(n):
        return pl.ds(pl.multiple_of(n * TILE, TILE), TILE)

    def turn(j):
        for k in range(Z):
            at_buf[j % X, :, pl.ds(k * SLOT, SLOT)] = a_buf[strip(j), k].T

    def multiply(j, q):
        h, part = j // X, j % X

        def body(n, carry):
            cols = columns(n)
            value = jnp.dot(
                at_buf[part], c_buf[:, :, cols].reshape(Z * SLOT, TILE),
                preferred_element_type=jnp.float32,
            ) * factor
            if (part, q) in ((1, 0), (2, 1)):
                value = value + relay[h, :, cols].astype(jnp.float32)
            if part == 3:
                value = value + near[h, 0, :, cols].astype(jnp.float32) + near[h, 1, :, cols].astype(jnp.float32)
                g_buf[g_rows(h, x), cols] = value.astype(jnp.bfloat16)
            else:
                t_buf[h, part, :, cols] = value.astype(jnp.bfloat16)
            return carry

        lax.fori_loop(q * 2, q * 2 + 2, body, 0)

    def t_wait(j, q):
        h, part = j // X, j % X
        if (part, q) in ((1, 0), (2, 1)):
            arrived(relay.at[h, :, side(q)], t_recv.at[h, 0, q])
        if part == 3:
            arrived(near.at[h, 0, :, side(q)], t_recv.at[h, 1, q])
            arrived(near.at[h, 1, :, side(q)], t_recv.at[h, 2, q])

    def t_put(j, q):
        h, part = j // X, j % X
        if part == 3:
            if q == 1:
                g_first(h)
            return
        way = (q, 0, 1)[part]
        dst = relay.at[h, :, side(q)] if part == 0 else near.at[h, way, :, side(q)]
        put(t_buf.at[h, part, :, side(q)], dst, t_send.at[h, part, q], t_recv.at[h, part, q], on_x(sign[way]))

    def term(j, q):
        t_wait(j, q)
        multiply(j, q)
        t_put(j, q)

    def own_rows():
        return jnp.concatenate([g_buf[g_rows(0, x), :], g_buf[g_rows(1, x), :]], axis=0)

    def keep(which, cols, value):
        value = value.astype(jnp.bfloat16)
        o_buf[which, 0, :, cols] = value[:PIECE]
        o_buf[which, 1, :, cols] = value[PIECE:]

    kept = []
    inverse = 1.0 / BLOCK

    def ship(which, cols, i):
        put(o_buf.at[which, other, :, cols], out_ref.at[which, zl, :, cols],
            o_send.at[which, i], o_recv.at[which, i], partner)
        copy = pltpu.make_async_copy(
            o_buf.at[which, zl, :, cols], out_ref.at[which, zl, :, cols], local_sem.at[4 + which * 5 + i])
        copy.start()
        kept.append(copy)

    def over_tiles(first, last, tile):
        def body(n, carry):
            tile(columns(n))
            return carry
        lax.fori_loop(first, last, body, 0)

    def left_tile(cols):
        keep(0, cols, inverse * lax.dot_general(
            own_rows(), g_buf[cols, :], (((1,), (1,)), ((), ())),
            preferred_element_type=jnp.float32))

    def left_part():
        over_tiles(0, 2, left_tile)
        ship(0, side(0), 0)

    def left_piece(i):
        cols = g_rows(1, target[i])
        left_tile(cols)
        ship(0, cols, 1 + i)

    def turn_own(h):
        rows = pl.ds(h * HALF, HALF)
        for i in (0, 1):
            gt_buf[pl.ds(i * PIECE, PIECE), rows] = g_buf[rows, g_rows(i, x)].T

    def right_part(h):
        rows = pl.ds(h * HALF, HALF)
        turn_own(h)

        def tile(cols):
            value = inverse * jnp.dot(gt_buf[:, rows], g_buf[rows, cols], preferred_element_type=jnp.float32)
            if h == 0:
                right_acc[:, cols] = value
            else:
                keep(1, cols, right_acc[:, cols] + value)
        for q in (0, 1):
            over_tiles(q * 2, q * 2 + 2, tile)
            if h == 1:
                ship(1, side(q), q)

    def lift_part(h):
        rows = pl.ds(h * HALF, HALF)

        def tile(cols):
            roots = l_buf[:, :, rows].reshape(2 * PIECE, HALF)
            value = jnp.dot(roots, g_buf[rows, cols], preferred_element_type=jnp.float32)
            if h == 0:
                lift_acc[:, cols] = value
            else:
                lift_buf[:, cols] = (lift_acc[:, cols] + value).astype(jnp.bfloat16)
        over_tiles(0, 4, tile)

    def update_part():
        def tile(cols):
            keep(2, cols, jnp.dot(
                lift_buf[...], r_buf[:, :, :, cols].reshape(BLOCK, TILE),
                preferred_element_type=jnp.float32))
        for q in (0, 1):
            over_tiles(q * 2, q * 2 + 2, tile)
            ship(2, side(q), q)

    put(c_ref.at[:, :, pl.ds(scaled(other, BLOCK), BLOCK)], c_chunk(zl, f),
        swap_send.at[0], swap_recv.at[0], partner)
    a_first(0)
    put(rr_ref.at[other], r_chunk(zl, x), swap_send.at[1], swap_recv.at[1], partner)
    r_first(rr_ref.at[zl], zl)
    arrived(c_chunk(other, f), swap_recv.at[0])
    c_first(c_ref.at[:, :, pl.ds(scaled(zl, BLOCK), BLOCK)], zl)
    c_first(c_chunk(other, f), other)
    local[0].wait()
    a_event(0)
    a_strips(0)
    for j in range(4):
        z_first(j)
    arrived(r_chunk(other, x), swap_recv.at[1])
    r_first(r_chunk(other, x), other)
    c_event(1, 0)
    c_event(1, 1)
    z_event(0, 1)
    z_event(1, 1)
    c_event(2, 0)
    z_event(2, 1)
    z_event(3, 1)
    c_event(2, 1)
    z_event(0, 2)
    z_event(1, 2)
    r_event(1)
    c_event(3, 0)
    a_first(1)
    z_event(2, 2)
    z_event(3, 2)
    c_event(3, 1)
    z_event(0, 3)
    z_event(1, 3)
    put(lr_ref.at[other], l_buf.at[zl], swap_send.at[2], swap_recv.at[2], partner)
    z_event(2, 3)
    z_event(3, 3)
    a_event(1)
    a_strips(1)
    z_first(4)
    z_first(5)
    z_first(6)
    local[1].wait()
    c_event(4, 0)
    c_event(4, 1)
    z_event(0, 4)
    turn(0)
    z_event(1, 4)
    turn(1)
    c_rest()
    term(0, 0)
    term(0, 1)
    z_event(4, 1)
    z_event(5, 1)
    z_first(7)
    term(1, 1)
    z_event(2, 4)
    turn(2)
    term(2, 0)
    z_event(3, 4)
    turn(3)
    z_event(6, 1)
    z_event(4, 2)
    z_event(5, 2)
    term(1, 0)
    z_event(7, 1)
    term(2, 1)
    z_event(4, 3)
    z_event(6, 2)
    z_event(5, 3)
    term(3, 0)
    term(3, 1)
    z_event(7, 2)
    z_event(4, 4)
    turn(4)
    term(4, 0)
    term(4, 1)
    z_event(5, 4)
    turn(5)
    term(5, 1)
    z_event(6, 3)
    z_event(7, 3)
    z_event(6, 4)
    turn(6)
    term(6, 0)
    g_event(0, 1)
    term(5, 0)
    term(6, 1)
    z_event(7, 4)
    turn(7)
    term(7, 0)
    term(7, 1)
    g_event(0, 2)
    left_part()
    right_part(0)
    local[2].wait()
    arrived(l_buf.at[other], swap_recv.at[2])
    lift_part(0)
    left_piece(3)
    g_event(1, 1)
    left_piece(2)
    left_piece(1)
    local[3].wait()
    r_event(2)
    g_event(1, 2)
    right_part(1)
    lift_part(1)
    update_part()
    left_piece(0)

    a_drain(0)
    a_drain(1)
    for copy in started:
        copy.wait_send()
    for copy in kept:
        copy.wait()
    for which in (1, 2):
        for q in (0, 1):
            arrived(out_ref.at[which, other, :, side(q)], o_recv.at[which, q])
    arrived(out_ref.at[0, other, :, side(0)], o_recv.at[0, 0])
    for i in range(X):
        arrived(out_ref.at[0, other, :, g_rows(1, target[i])], o_recv.at[0, 1 + i])


def on_device(activations, cotangent, left_root, right_root):
    tokens = cotangent.shape[0]
    factor = float(tokens * lax.axis_size("dp") * lax.axis_size("fsdp")) ** (-0.5)
    bf16 = jnp.bfloat16
    dma = pltpu.SemaphoreType.DMA
    anywhere = pl.BlockSpec(memory_space=pltpu.HBM)
    out = pl.pallas_call(
        functools.partial(kernel, factor),
        out_shape=jax.ShapeDtypeStruct((3, 2, PIECE, BLOCK), bf16),
        in_specs=[anywhere] * 4,
        out_specs=anywhere,
        scratch_shapes=[
            pltpu.VMEM((SLOT, BLOCK), bf16),
            pltpu.VMEM((2 * X, Z, SLOT, PIECE), bf16),
            pltpu.VMEM((Z, SLOT, BLOCK), bf16),
            pltpu.VMEM((BLOCK, BLOCK), bf16),
            pltpu.VMEM((2, X, PIECE, BLOCK), bf16),
            pltpu.VMEM((2, PIECE, BLOCK), bf16),
            pltpu.VMEM((X, PIECE, Z * SLOT), bf16),
            pltpu.VMEM((2, 3, PIECE, BLOCK), bf16),
            pltpu.VMEM((2, PIECE, BLOCK), bf16),
            pltpu.VMEM((2, 2, PIECE, BLOCK), bf16),
            pltpu.VMEM((2 * PIECE, BLOCK), bf16),
            pltpu.VMEM((2 * PIECE, BLOCK), bf16),
            pltpu.VMEM((2 * PIECE, BLOCK), jnp.float32),
            pltpu.VMEM((2 * PIECE, BLOCK), jnp.float32),
            pltpu.VMEM((3, 2, PIECE, BLOCK), bf16),
            dma((20,)), dma((3,)), dma((3,)),
            dma((2, F)), dma((2, F)),
            dma((2, 2, 5)), dma((2, 2, 5)), dma((2, 2, 5)), dma((2, 2, 5)),
            dma((2, 8, 5)), dma((2, 8, 5)),
            dma((2, 3, 2)), dma((2, 3, 2)),
            dma((2, 2, 2, 3)), dma((2, 2, 2, 3)),
            dma((2, 2, 3)), dma((2, 2, 3)),
            dma((3, 5)), dma((3, 5)),
        ],
        compiler_params=pltpu.CompilerParams(
            collective_id=0, has_side_effects=True, vmem_limit_bytes=40 * 1024 * 1024
        ),
        cost_estimate=pl.CostEstimate(
            flops=6 * 2**30, bytes_accessed=8 * 2**20, transcendentals=0),
    )(*(
        pltpu.with_memory_space_constraint(value, pltpu.HBM)
        for value in (
            activations,
            cotangent.reshape(T, ROWS, 2 * BLOCK),
            left_root.reshape(2, PIECE, BLOCK),
            right_root.reshape(2, PIECE, BLOCK),
        )
    ))
    shape = left_root.shape
    return (
        out[0].reshape(shape).astype(jnp.float32),
        out[1].reshape(shape).astype(jnp.float32),
        out[2].reshape(shape),
    )


def solution(mesh):
    return jax.shard_map(
        on_device,
        mesh=mesh,
        in_specs=(
            P(("dp", "fsdp", "tensor"), None),
            P(("dp", "fsdp"), "tensor"),
            P("fsdp", "tensor", "dp", None),
            P("fsdp", "tensor", "dp", None),
        ),
        out_specs=(
            P("fsdp", "tensor", "dp", None),
            P("fsdp", "tensor", "dp", None),
            P("fsdp", "tensor", "dp", None),
        ),
        check_vma=False,
    )
```

```python
import functools

import jax
import jax.numpy as jnp
from jax import lax
from jax.experimental import pallas as pl
from jax.experimental.pallas import tpu as pltpu
from jax.sharding import PartitionSpec as P

MESH = pl.DeviceIdType.MESH
X, Y, Z, CORES = 4, 8, 8, 2
F = Y * CORES
T = Z // 2
PIECE = 128
BLOCK = 1024
HALF = BLOCK // 2
ROWS = 16
SLOT = F * ROWS
TILE = 256


def mod(value, size):
    return lax.rem(value + 2 * size, size)


def scaled(index, size):
    return pl.multiple_of(index * size, size)


def kernel(
    factor,
    a_ref, c_ref, lr_ref, rr_ref,
    out_ref,
    stage, a_buf, c_buf, g_buf, r_buf, l_buf, at_buf, t_buf, relay, near, gt_buf, lift_buf,
    right_acc, lift_acc, o_buf,
    local_sem, swap_send, swap_recv,
    a_send, a_recv, c_send, c_recv, sib_send, sib_recv,
    z_send, z_recv, t_send, t_recv, g_send, g_recv, r_send, r_recv, o_send, o_recv,
):
    m = lax.axis_index("dp")
    f = lax.axis_index("fsdp")
    t = lax.axis_index("tensor")
    zl, x = lax.div(m, X), lax.rem(m, X)
    y, core = lax.div(f, CORES), lax.rem(f, CORES)
    z = 2 * t + zl
    other = 1 - zl

    def on_x(step):
        return (zl * X + mod(x + step, X), f, t)

    def on_y(step):
        return (m, mod(y + step, Y) * CORES + core, t)

    def on_z(step):
        there = mod(z + step, Z)
        return (lax.rem(there, 2) * X + x, f, lax.div(there, 2))

    def slot_of(there):
        return lax.rem(there, 2) * T + lax.div(there, 2)

    sibling = (m, y * CORES + 1 - core, t)
    partner = (other * X + x, f, t)
    sign = (1, -1)
    slot = slot_of(z)
    my_rows = scaled(f, ROWS)

    started = []

    def put(src, dst, send, recv, device):
        copy = pltpu.make_async_remote_copy(
            src_ref=src, dst_ref=dst, send_sem=send, recv_sem=recv,
            device_id=device, device_id_type=MESH,
        )
        copy.start()
        started.append(copy)

    def arrived(dst, recv):
        pltpu.make_async_remote_copy(
            src_ref=dst, dst_ref=dst, send_sem=recv, recv_sem=recv,
            device_id=sibling, device_id_type=MESH,
        ).wait_recv()

    barrier = pltpu.get_barrier_semaphore()

    def greet(d, carry):
        pl.semaphore_signal(barrier, inc=1, device_id=(m, mod(f + d, F), t), device_id_type=MESH)
        return carry

    for device in (on_z(1), on_z(-1), on_x(1), on_x(-1)):
        pl.semaphore_signal(barrier, inc=1, device_id=device, device_id_type=MESH)
    lax.fori_loop(1, F, greet, 0)

    local = [
        pltpu.make_async_copy(
            a_ref.at[:, pl.ds(scaled(f, BLOCK), BLOCK)],
            stage.at[pl.ds(my_rows, ROWS), :], local_sem.at[0]),
        pltpu.make_async_copy(
            c_ref.at[:, :, pl.ds(scaled(zl, BLOCK), BLOCK)],
            c_buf.at[pl.ds(zl * T, T), pl.ds(my_rows, ROWS), :], local_sem.at[1]),
        pltpu.make_async_copy(lr_ref.at[zl], l_buf.at[zl], local_sem.at[2]),
        pltpu.make_async_copy(rr_ref.at[zl], r_buf.at[zl, x], local_sem.at[3]),
    ]
    for copy in local:
        copy.start()
    pl.semaphore_wait(barrier, F - 1 + 4)

    def a_copy(part, d):
        to = mod(f + d, F)
        start = pl.multiple_of(to * BLOCK + part * HALF, HALF)
        return pltpu.make_async_remote_copy(
            src_ref=a_ref.at[:, pl.ds(start, HALF)],
            dst_ref=stage.at[pl.ds(my_rows, ROWS), pl.ds(part * HALF, HALF)],
            send_sem=a_send.at[part, d], recv_sem=a_recv.at[part, d],
            device_id=(m, to, t), device_id_type=MESH)

    def a_first(part):
        def body(d, carry):
            a_copy(part, d).start()
            return carry
        lax.fori_loop(1, F, body, 0)

    def a_event(part):
        def body(d, carry):
            rows = pl.ds(scaled(mod(f - d, F), ROWS), ROWS)
            arrived(stage.at[rows, pl.ds(part * HALF, HALF)], a_recv.at[part, d])
            return carry
        lax.fori_loop(1, F, body, 0)

    def a_drain(part):
        def body(d, carry):
            a_copy(part, d).wait_send()
            return carry
        lax.fori_loop(1, F, body, 0)

    def a_strips(part):
        for i in range(part * X, part * X + X):
            a_buf[i, slot] = stage[:, i * PIECE:(i + 1) * PIECE]

    def c_chunk(half, owner):
        return c_buf.at[pl.ds(half * T, T), pl.ds(scaled(owner, ROWS), ROWS), :]

    def c_share(src, half, owner, way, step):
        put(src, c_chunk(half, owner), sib_send.at[half, way, step], sib_recv.at[half, way, step], sibling)

    def c_first(src, half):
        for way in (0, 1):
            put(src, c_chunk(half, f), c_send.at[way, half, 0], c_recv.at[way, half, 1], on_y(sign[way]))
        c_share(src, half, f, 0, 0)

    def c_event(step, half):
        for way in (0, 1):
            if step == Y // 2 and way != half:
                continue
            owner = mod(y - sign[way] * step, Y) * CORES + core
            chunk = c_chunk(half, owner)
            arrived(chunk, c_recv.at[way, half, step])
            if step < Y // 2 - 1 or (step == Y // 2 - 1 and way == half):
                put(chunk, chunk, c_send.at[way, half, step], c_recv.at[way, half, step + 1],
                    on_y(sign[way]))
            c_share(chunk, half, owner, way, step)

    def c_rest():
        for step in range(Y // 2 + 1):
            for half in (0, 1):
                for way in (0, 1):
                    if (step == Y // 2 and way != half) or (step == 0 and way == 1):
                        continue
                    owner = mod(y - sign[way] * step, Y) * CORES + 1 - core
                    arrived(c_chunk(half, owner), sib_recv.at[half, way, step])

    target = (mod(x + 2, X), mod(x + 1, X), mod(x - 1, X), x)

    def strip(j):
        return (j // X) * X + target[j % X]

    def z_put(j, way, step, owner):
        ref = a_buf.at[strip(j), owner]
        put(ref, ref, z_send.at[way, j, step], z_recv.at[way, j, step + 1], on_z(sign[way]))

    def z_first(j):
        for way in (0, 1):
            z_put(j, way, 0, slot)

    def z_event(j, step):
        for way in (0, 1):
            if step == Z // 2 and way != j % 2:
                continue
            owner = slot_of(mod(z - sign[way] * step, Z))
            arrived(a_buf.at[strip(j), owner], z_recv.at[way, j, step])
            if step < Z // 2 - 1 or (step == Z // 2 - 1 and way == j % 2):
                z_put(j, way, step, owner)

    def x_first(src_of, dst_of, send, recv, half):
        for way in (0, 1):
            put(src_of, dst_of, send.at[way, half, 0], recv.at[way, half, 1], on_x(sign[way]))

    def x_ring(ref_of, send, recv, step):
        for turned in (0, 1):
            for way in (0, 1):
                half = (way + turned) % 2
                if step == X // 2 and way != half:
                    continue
                ref = ref_of(half, mod(x - sign[way] * step, X))
                arrived(ref, recv.at[way, half, step])
                if step < X // 2 - 1 or (step == X // 2 - 1 and way == half):
                    put(ref, ref, send.at[way, half, step], recv.at[way, half, step + 1], on_x(sign[way]))

    def r_chunk(half, owner):
        return r_buf.at[half, owner]

    def r_first(src, half):
        x_first(src, r_chunk(half, x), r_send, r_recv, half)

    def r_event(step):
        x_ring(r_chunk, r_send, r_recv, step)

    def g_rows(h, owner):
        return pl.ds(pl.multiple_of((h * X + owner) * PIECE, PIECE), PIECE)

    def side(q):
        return pl.ds(q * HALF, HALF)

    def g_chunk(h):
        return lambda q, owner: g_buf.at[g_rows(h, owner), side(q)]

    def g_first(h):
        for q in (0, 1):
            for way in (0, 1):
                half = (way + q) % 2
                ref = g_chunk(h)(half, x)
                put(ref, ref, g_send.at[h, way, half, 0], g_recv.at[h, way, half, 1], on_x(sign[way]))

    def g_event(h, step):
        x_ring(g_chunk(h), g_send.at[h], g_recv.at[h], step)

    def columns(n):
        return pl.ds(pl.multiple_of(n * TILE, TILE), TILE)

    def turn(j):
        for k in range(Z):
            at_buf[j % X, :, pl.ds(k * SLOT, SLOT)] = a_buf[strip(j), k].T

    def multiply(j, q):
        h, part = j // X, j % X

        def body(n, carry):
            cols = columns(n)
            value = jnp.dot(
                at_buf[part], c_buf[:, :, cols].reshape(Z * SLOT, TILE),
                preferred_element_type=jnp.float32,
            ) * factor
            if (part, q) in ((1, 0), (2, 1)):
                value = value + relay[h, :, cols].astype(jnp.float32)
            if part == 3:
                value = value + near[h, 0, :, cols].astype(jnp.float32) + near[h, 1, :, cols].astype(jnp.float32)
                g_buf[g_rows(h, x), cols] = value.astype(jnp.bfloat16)
            else:
                t_buf[h, part, :, cols] = value.astype(jnp.bfloat16)
            return carry

        lax.fori_loop(q * 2, q * 2 + 2, body, 0)

    def t_wait(j, q):
        h, part = j // X, j % X
        if (part, q) in ((1, 0), (2, 1)):
            arrived(relay.at[h, :, side(q)], t_recv.at[h, 0, q])
        if part == 3:
            arrived(near.at[h, 0, :, side(q)], t_recv.at[h, 1, q])
            arrived(near.at[h, 1, :, side(q)], t_recv.at[h, 2, q])

    def t_put(j, q):
        h, part = j // X, j % X
        if part == 3:
            if q == 1:
                g_first(h)
            return
        way = (q, 0, 1)[part]
        dst = relay.at[h, :, side(q)] if part == 0 else near.at[h, way, :, side(q)]
        put(t_buf.at[h, part, :, side(q)], dst, t_send.at[h, part, q], t_recv.at[h, part, q], on_x(sign[way]))

    def term(j, q):
        t_wait(j, q)
        multiply(j, q)
        t_put(j, q)

    def own_rows():
        return jnp.concatenate([g_buf[g_rows(0, x), :], g_buf[g_rows(1, x), :]], axis=0)

    def keep(which, cols, value):
        value = value.astype(jnp.bfloat16)
        o_buf[which, 0, :, cols] = value[:PIECE]
        o_buf[which, 1, :, cols] = value[PIECE:]

    kept = []
    inverse = 1.0 / BLOCK

    def ship(which, cols, i):
        put(o_buf.at[which, other, :, cols], out_ref.at[which, zl, :, cols],
            o_send.at[which, i], o_recv.at[which, i], partner)
        copy = pltpu.make_async_copy(
            o_buf.at[which, zl, :, cols], out_ref.at[which, zl, :, cols], local_sem.at[4 + which * 5 + i])
        copy.start()
        kept.append(copy)

    def over_tiles(first, last, tile):
        def body(n, carry):
            tile(columns(n))
            return carry
        lax.fori_loop(first, last, body, 0)

    def left_tile(cols):
        keep(0, cols, inverse * lax.dot_general(
            own_rows(), g_buf[cols, :], (((1,), (1,)), ((), ())),
            preferred_element_type=jnp.float32))

    def left_part():
        over_tiles(0, 2, left_tile)
        ship(0, side(0), 0)

    def left_piece(i):
        cols = g_rows(1, target[i])
        left_tile(cols)
        ship(0, cols, 1 + i)

    def turn_own(h):
        rows = pl.ds(h * HALF, HALF)
        for i in (0, 1):
            gt_buf[pl.ds(i * PIECE, PIECE), rows] = g_buf[rows, g_rows(i, x)].T

    def right_part(h):
        rows = pl.ds(h * HALF, HALF)
        turn_own(h)

        def tile(cols):
            value = inverse * jnp.dot(gt_buf[:, rows], g_buf[rows, cols], preferred_element_type=jnp.float32)
            if h == 0:
                right_acc[:, cols] = value
            else:
                keep(1, cols, right_acc[:, cols] + value)
        for q in (0, 1):
            over_tiles(q * 2, q * 2 + 2, tile)
            if h == 1:
                ship(1, side(q), q)

    def lift_part(h):
        rows = pl.ds(h * HALF, HALF)

        def tile(cols):
            roots = l_buf[:, :, rows].reshape(2 * PIECE, HALF)
            value = jnp.dot(roots, g_buf[rows, cols], preferred_element_type=jnp.float32)
            if h == 0:
                lift_acc[:, cols] = value
            else:
                lift_buf[:, cols] = (lift_acc[:, cols] + value).astype(jnp.bfloat16)
        over_tiles(0, 4, tile)

    def update_part():
        def tile(cols):
            keep(2, cols, jnp.dot(
                lift_buf[...], r_buf[:, :, :, cols].reshape(BLOCK, TILE),
                preferred_element_type=jnp.float32))
        for q in (0, 1):
            over_tiles(q * 2, q * 2 + 2, tile)
            ship(2, side(q), q)

    put(c_ref.at[:, :, pl.ds(scaled(other, BLOCK), BLOCK)], c_chunk(zl, f),
        swap_send.at[0], swap_recv.at[0], partner)
    a_first(0)
    put(rr_ref.at[other], r_chunk(zl, x), swap_send.at[1], swap_recv.at[1], partner)
    r_first(rr_ref.at[zl], zl)
    arrived(c_chunk(other, f), swap_recv.at[0])
    c_first(c_ref.at[:, :, pl.ds(scaled(zl, BLOCK), BLOCK)], zl)
    c_first(c_chunk(other, f), other)
    local[0].wait()
    a_event(0)
    a_strips(0)
    for j in range(4):
        z_first(j)
    arrived(r_chunk(other, x), swap_recv.at[1])
    r_first(r_chunk(other, x), other)
    c_event(1, 0)
    c_event(1, 1)
    z_event(0, 1)
    z_event(1, 1)
    c_event(2, 0)
    z_event(2, 1)
    z_event(3, 1)
    c_event(2, 1)
    z_event(0, 2)
    z_event(1, 2)
    r_event(1)
    c_event(3, 0)
    a_first(1)
    z_event(2, 2)
    z_event(3, 2)
    c_event(3, 1)
    z_event(0, 3)
    z_event(1, 3)
    put(lr_ref.at[other], l_buf.at[zl], swap_send.at[2], swap_recv.at[2], partner)
    z_event(2, 3)
    z_event(3, 3)
    a_event(1)
    a_strips(1)
    z_first(4)
    z_first(5)
    z_first(6)
    local[1].wait()
    c_event(4, 0)
    c_event(4, 1)
    z_event(0, 4)
    turn(0)
    z_event(1, 4)
    turn(1)
    c_rest()
    term(0, 0)
    term(0, 1)
    z_event(4, 1)
    z_event(5, 1)
    z_first(7)
    term(1, 1)
    z_event(2, 4)
    turn(2)
    term(2, 0)
    z_event(3, 4)
    turn(3)
    z_event(6, 1)
    z_event(4, 2)
    z_event(5, 2)
    term(1, 0)
    z_event(7, 1)
    term(2, 1)
    z_event(4, 3)
    z_event(6, 2)
    z_event(5, 3)
    z_event(7, 2)
    z_event(4, 4)
    turn(4)
    term(4, 0)
    term(4, 1)
    term(3, 0)
    term(3, 1)
    z_event(5, 4)
    turn(5)
    term(5, 1)
    z_event(6, 3)
    z_event(7, 3)
    z_event(6, 4)
    turn(6)
    term(6, 0)
    g_event(0, 1)
    term(5, 0)
    term(6, 1)
    z_event(7, 4)
    turn(7)
    term(7, 0)
    term(7, 1)
    g_event(0, 2)
    left_part()
    right_part(0)
    local[2].wait()
    arrived(l_buf.at[other], swap_recv.at[2])
    lift_part(0)
    left_piece(3)
    g_event(1, 1)
    left_piece(2)
    left_piece(1)
    local[3].wait()
    r_event(2)
    g_event(1, 2)
    right_part(1)
    lift_part(1)
    update_part()
    left_piece(0)

    a_drain(0)
    a_drain(1)
    for copy in started:
        copy.wait_send()
    for copy in kept:
        copy.wait()
    for which in (1, 2):
        for q in (0, 1):
            arrived(out_ref.at[which, other, :, side(q)], o_recv.at[which, q])
    arrived(out_ref.at[0, other, :, side(0)], o_recv.at[0, 0])
    for i in range(X):
        arrived(out_ref.at[0, other, :, g_rows(1, target[i])], o_recv.at[0, 1 + i])


def on_device(activations, cotangent, left_root, right_root):
    tokens = cotangent.shape[0]
    factor = float(tokens * lax.axis_size("dp") * lax.axis_size("fsdp")) ** (-0.5)
    bf16 = jnp.bfloat16
    dma = pltpu.SemaphoreType.DMA
    anywhere = pl.BlockSpec(memory_space=pltpu.HBM)
    out = pl.pallas_call(
        functools.partial(kernel, factor),
        out_shape=jax.ShapeDtypeStruct((3, 2, PIECE, BLOCK), bf16),
        in_specs=[anywhere] * 4,
        out_specs=anywhere,
        scratch_shapes=[
            pltpu.VMEM((SLOT, BLOCK), bf16),
            pltpu.VMEM((2 * X, Z, SLOT, PIECE), bf16),
            pltpu.VMEM((Z, SLOT, BLOCK), bf16),
            pltpu.VMEM((BLOCK, BLOCK), bf16),
            pltpu.VMEM((2, X, PIECE, BLOCK), bf16),
            pltpu.VMEM((2, PIECE, BLOCK), bf16),
            pltpu.VMEM((X, PIECE, Z * SLOT), bf16),
            pltpu.VMEM((2, 3, PIECE, BLOCK), bf16),
            pltpu.VMEM((2, PIECE, BLOCK), bf16),
            pltpu.VMEM((2, 2, PIECE, BLOCK), bf16),
            pltpu.VMEM((2 * PIECE, BLOCK), bf16),
            pltpu.VMEM((2 * PIECE, BLOCK), bf16),
            pltpu.VMEM((2 * PIECE, BLOCK), jnp.float32),
            pltpu.VMEM((2 * PIECE, BLOCK), jnp.float32),
            pltpu.VMEM((3, 2, PIECE, BLOCK), bf16),
            dma((20,)), dma((3,)), dma((3,)),
            dma((2, F)), dma((2, F)),
            dma((2, 2, 5)), dma((2, 2, 5)), dma((2, 2, 5)), dma((2, 2, 5)),
            dma((2, 8, 5)), dma((2, 8, 5)),
            dma((2, 3, 2)), dma((2, 3, 2)),
            dma((2, 2, 2, 3)), dma((2, 2, 2, 3)),
            dma((2, 2, 3)), dma((2, 2, 3)),
            dma((3, 5)), dma((3, 5)),
        ],
        compiler_params=pltpu.CompilerParams(
            collective_id=0, has_side_effects=True, vmem_limit_bytes=40 * 1024 * 1024
        ),
        cost_estimate=pl.CostEstimate(
            flops=6 * 2**30, bytes_accessed=8 * 2**20, transcendentals=0),
    )(*(
        pltpu.with_memory_space_constraint(value, pltpu.HBM)
        for value in (
            activations,
            cotangent.reshape(T, ROWS, 2 * BLOCK),
            left_root.reshape(2, PIECE, BLOCK),
            right_root.reshape(2, PIECE, BLOCK),
        )
    ))
    shape = left_root.shape
    return (
        out[0].reshape(shape).astype(jnp.float32),
        out[1].reshape(shape).astype(jnp.float32),
        out[2].reshape(shape),
    )


def solution(mesh):
    return jax.shard_map(
        on_device,
        mesh=mesh,
        in_specs=(
            P(("dp", "fsdp", "tensor"), None),
            P(("dp", "fsdp"), "tensor"),
            P("fsdp", "tensor", "dp", None),
            P("fsdp", "tensor", "dp", None),
        ),
        out_specs=(
            P("fsdp", "tensor", "dp", None),
            P("fsdp", "tensor", "dp", None),
            P("fsdp", "tensor", "dp", None),
        ),
        check_vma=False,
    )
```
